32 devices in a mesh: space: 4 (over x, core), frame: 8 (over z, y).
Axes of the slice: x: 2, y: 2, z: 4, core: 2. Of those that a mesh axis runs over, the one named last changes fastest.
Arguments:
- latent: bfloat16 [8, 2048, 1024], P('frame', 'space'), may hold values from -6 to 6
- cond: float32 [3, 1024], replicated, may hold values from -3 to 3
- w_qkv: bfloat16 [1024, 3072], replicated
- w_out: bfloat16 [1024, 1024], replicated, may hold values from -0.1875 to 0.1875
- slot: int32 [2048], P('space'), may hold values from 0 to 511, as said below
- neighbours: int32 [16, 4], P('space'), may hold values from 0 to 15, as said below
- counts: int32 [16], P('space'), may hold values from 1 to 4
Outputs:
- updated: bfloat16 [8, 2048, 1024], P('frame', 'space')
The draws below stay inside these ranges and needn't reach their ends.
Inputs may be any that keep to these rules, and one draw needn't show every extreme that they name: `slot`: each aligned group of 512 entries is a permutation of its range. `neighbours`: row b lists distinct blocks (b + o) mod 16 with -4 <= o <= 4, the first being b itself.
All inputs are finite; a program needn't handle non-finite values.
Results may differ from the reference program's by a relative error of at most 0.0052.
Values may be sent and summed in bfloat16 or wider, within the bound.
A program may use at most 64 MiB of HBM per device.

```python
import jax
import jax.numpy as jnp
from jax import lax

D = 1024
HEADS = 8
BLOCK = 128
MAXNB = 4
BLK_DEV = 4
TOK_DEV = 512
NBLK = 16
NTOK = 2048
FRAMES = 8
CLIP = 8


def draw_w_qkv(key, part):
    first = jax.random.fold_in(key, 0)
    base = jax.random.normal(first, (D, 3 * D), jnp.float32) / jnp.sqrt(jnp.float32(D))
    return base.astype(jnp.bfloat16)


def draw_slot(key, part):
    groups = jax.random.split(key, NTOK // TOK_DEV)
    perms = jax.vmap(lambda k: jax.random.permutation(k, TOK_DEV))(groups)
    return perms.reshape(-1).astype(jnp.int32)


def draw_neighbours(key, part):
    rows = jax.random.split(jax.random.fold_in(key, 11), NBLK)
    picks = jax.vmap(lambda k: jax.random.permutation(k, 2 * BLK_DEV)[:MAXNB - 1])(rows)
    offsets = jnp.concatenate([jnp.arange(-BLK_DEV, 0, dtype=jnp.int32), jnp.arange(1, BLK_DEV + 1, dtype=jnp.int32)])
    chosen = jnp.concatenate([jnp.zeros((NBLK, 1), jnp.int32), offsets[picks]], axis=1)
    return jnp.mod(jnp.arange(NBLK, dtype=jnp.int32)[:, None] + chosen, NBLK).astype(jnp.int32)


def draw_counts(key, part):
    first, second = jax.random.split(jax.random.fold_in(key, 23))
    device_top = jax.random.randint(first, (NBLK // BLK_DEV,), 1, MAXNB + 1)
    tops = jnp.repeat(device_top, BLK_DEV)
    drawn = jax.random.randint(second, (NBLK,), 1, tops + 1)
    return drawn.at[0].set(MAXNB).astype(jnp.int32)


def levels(own_key, dims, pieces, smallest, largest):
    def one(axis_at, shards_of):
        steps = jax.random.uniform(jax.random.fold_in(jax.random.fold_in(own_key, 6), axis_at), (shards_of,), jnp.float32, smallest / len(pieces), largest / len(pieces))
        return jnp.repeat(jnp.exp(steps), dims[axis_at] // shards_of).reshape((-1,) + (1,) * (len(dims) - axis_at - 1))

    level = one(*pieces[0])
    for cut in pieces[1:]:
        level = level * one(*cut)
    return level


def normal_values(key, extent, width, most, shards=(), kind=jnp.bfloat16):
    array = jax.random.normal(key, extent, jnp.float32) * width
    if len(shards) > 0:
        array = levels(key, extent, shards, -0.22, 0.18) * array
    return jnp.clip(array, min=-most, max=most).astype(kind)


def setup_inputs(seed: int = 0) -> dict:
    key_list = jax.random.split(jax.random.key(seed), 8)
    latent = normal_values(key_list[0], (FRAMES, NTOK, D), 1.0, 6.0, ((0, 8), (1, 4)))
    cond = normal_values(key_list[1], (3, D), 0.7, 3.0, (), jnp.float32)
    w_qkv = draw_w_qkv(jax.random.fold_in(key_list[7], 71), 0)
    w_out = normal_values(key_list[3], (D, D), D ** -0.5, 0.1875)
    slot = draw_slot(jax.random.fold_in(key_list[7], 71), 0)
    neighbours = draw_neighbours(jax.random.fold_in(key_list[7], 71), 0)
    counts = draw_counts(jax.random.fold_in(key_list[7], 71), 0)
    return dict(latent=latent, cond=cond, w_qkv=w_qkv, w_out=w_out, slot=slot, neighbours=neighbours, counts=counts)


def softmax_last(scores):
    top = lax.optimization_barrier(jnp.max(scores, axis=-1, keepdims=True))
    expo = jnp.exp(scores - top)
    return expo / lax.optimization_barrier(jnp.sum(expo, axis=-1, keepdims=True))

def reference(latent, cond, w_qkv, w_out, slot, neighbours, counts):
    head_dim = D // HEADS
    sheads = HEADS // 2
    half = D // 2
    scale = 1.0 / jnp.sqrt(jnp.float32(head_dim))
    x_full = latent.astype(jnp.float32)

    def project(frame_rows):
        centred = frame_rows - lax.optimization_barrier(jnp.mean(frame_rows, axis=-1, keepdims=True))
        normed = centred * lax.rsqrt(lax.optimization_barrier(jnp.mean(centred * centred, axis=-1, keepdims=True)) + 1e-06)
        modulated = (normed * (1.0 + cond[1]) + cond[0]).astype(jnp.bfloat16)
        return jnp.dot(modulated, w_qkv, preferred_element_type=jnp.float32).astype(jnp.bfloat16)
    projected = lax.map(project, x_full)
    order = jnp.arange(NTOK, dtype=jnp.int32) // TOK_DEV * TOK_DEV + slot.astype(jnp.int32)
    valid = jnp.arange(MAXNB, dtype=jnp.int32)[None, :] < counts[:, None]

    def spatial_frame(proj):
        ranked = proj[order]
        q_blocks = ranked[:, :half].reshape(NBLK, BLOCK, sheads, head_dim)
        k_blocks = ranked[:, D:D + half].reshape(NBLK, BLOCK, sheads, head_dim)
        v_blocks = ranked[:, 2 * D:2 * D + half].reshape(NBLK, BLOCK, sheads, head_dim)

        def one_block(items):
            query, ids, usable = items
            keys = k_blocks[ids].reshape(MAXNB * BLOCK, sheads, head_dim).astype(jnp.float32)
            vals = v_blocks[ids].reshape(MAXNB * BLOCK, sheads, head_dim).astype(jnp.float32)
            scores = jnp.einsum('qhd,khd->hqk', query.astype(jnp.float32), keys, precision=lax.Precision.HIGHEST) * scale
            keep = jnp.repeat(usable, BLOCK)[None, None, :]
            scores = jnp.where(keep, scores, -jnp.inf)
            weights = softmax_last(scores).astype(jnp.bfloat16).astype(jnp.float32)
            result = jnp.einsum('hqk,khd->qhd', weights, vals, precision=lax.Precision.HIGHEST)
            return result.astype(jnp.bfloat16).reshape(BLOCK, half)
        block_out = lax.map(one_block, (q_blocks, neighbours, valid)).reshape(NTOK, half)
        return jnp.zeros((NTOK, half), jnp.bfloat16).at[order].set(block_out)
    spatial = lax.map(spatial_frame, projected)
    clip_of = jnp.arange(FRAMES, dtype=jnp.int32) // CLIP
    same_clip = clip_of[:, None] == clip_of[None, :]

    def temporal_head(head):
        lo = half + head * head_dim
        t_query = lax.dynamic_slice_in_dim(projected, lo, head_dim, 2).astype(jnp.float32)
        t_key = lax.dynamic_slice_in_dim(projected, D + lo, head_dim, 2).astype(jnp.float32)
        t_val = lax.dynamic_slice_in_dim(projected, 2 * D + lo, head_dim, 2).astype(jnp.float32)
        t_scores = jnp.einsum('ftd,gtd->tfg', t_query, t_key, precision=lax.Precision.HIGHEST) * scale
        t_scores = jnp.where(same_clip[None], t_scores, -jnp.inf)
        t_weights = softmax_last(t_scores)
        result = jnp.einsum('tfg,gtd->ftd', t_weights, t_val, precision=lax.Precision.HIGHEST)
        return result.astype(jnp.bfloat16)
    per_head = lax.map(temporal_head, jnp.arange(sheads, dtype=jnp.int32))
    temporal = jnp.transpose(per_head, (1, 2, 0, 3)).reshape(FRAMES, NTOK, half)
    joined = jnp.concatenate([spatial, temporal], axis=-1)

    def finish(items):
        heads_out, rows = items
        mixed = jnp.dot(heads_out, w_out, preferred_element_type=jnp.float32)
        return (rows + cond[2] * mixed).astype(jnp.bfloat16)
    return lax.map(finish, (joined, x_full))
```

```python
import functools

import jax
import jax.numpy as jnp
from jax import lax
from jax.experimental import pallas as pl
from jax.experimental.pallas import tpu as pltpu
from jax.sharding import PartitionSpec as P

HEADS = 8
MAXNB = 4
MESH = pl.DeviceIdType.MESH
F32 = jnp.float32
BF16 = jnp.bfloat16
CHUNK = 16


def modulate(rows, cond_ref):
    rows = rows.astype(F32)
    centred = rows - jnp.mean(rows, axis=-1, keepdims=True)
    normed = centred * lax.rsqrt(jnp.mean(centred * centred, axis=-1, keepdims=True) + 1e-06)
    return (normed * (1.0 + cond_ref[1:2, :]) + cond_ref[0:1, :]).astype(BF16)


def dot(a, b):
    return jnp.dot(a, b, preferred_element_type=F32)


def dot_t(a, b):
    return lax.dot_general(a, b, (((1,), (1,)), ((), ())), preferred_element_type=F32)


def kernel(
    clip,
    lat_hbm,
    cond_ref,
    wqkv_hbm,
    wout_hbm,
    slot_ref,
    nb_ref,
    cnt_ref,
    out_hbm,
    lat,
    wqkv,
    wout,
    grp,
    mod,
    ranked,
    query,
    kwin,
    vwin,
    place,
    block_out,
    sp_mixed,
    t_out,
    tmp,
    out_v,
    local_sem,
    own_sem,
    lat_send,
    lat_recv,
    halo_send,
    halo_recv,
    ret_send,
    ret_recv,
    out_sem,
):
    space_total = lax.axis_size("space")
    me_s = lax.axis_index("space")
    me_f = lax.axis_index("frame")
    rank = lax.rem(me_f, clip)
    base = me_f - rank
    left = lax.rem(me_s + space_total - 1, space_total)
    right = lax.rem(me_s + 1, space_total)
    per, width = lat.shape[1], lat.shape[2]
    tokens = clip * per
    half = width // 2
    head_dim = width // HEADS
    sheads = HEADS // 2
    blocks, block_len = slot_ref.shape
    chunks = per // CHUNK
    rows = clip * CHUNK
    scale = 1.0 / (head_dim**0.5)

    def peer_of(p):
        return lax.rem(rank + p, clip)

    lat_in = pltpu.make_async_copy(lat_hbm, lat, local_sem.at[0])
    wqkv_in = pltpu.make_async_copy(wqkv_hbm, wqkv, local_sem.at[1])
    wout_in = pltpu.make_async_copy(wout_hbm, wout, local_sem.at[2])

    def own_copy(c):
        return pltpu.make_async_copy(
            lat_hbm.at[rank, pl.ds(pl.multiple_of(c * CHUNK, CHUNK), CHUNK)],
            grp.at[c, rank],
            own_sem.at[c],
        )

    def lat_copy(c, peer, slot):
        return pltpu.make_async_remote_copy(
            src_ref=lat_hbm.at[peer, pl.ds(pl.multiple_of(c * CHUNK, CHUNK), CHUNK)],
            dst_ref=grp.at[c, slot],
            send_sem=lat_send.at[c, peer],
            recv_sem=lat_recv.at[c, slot],
            device_id={"frame": base + peer},
            device_id_type=MESH,
        )

    def ret_copy(c, peer, slot):
        return pltpu.make_async_remote_copy(
            src_ref=t_out.at[c, peer],
            dst_ref=tmp.at[c, slot],
            send_sem=ret_send.at[c, peer],
            recv_sem=ret_recv.at[c, slot],
            device_id={"frame": base + peer},
            device_id_type=MESH,
        )

    def halo_copy(win, kind, side):
        return pltpu.make_async_remote_copy(
            src_ref=win.at[pl.ds(blocks, blocks)],
            dst_ref=win.at[pl.ds(2 * blocks * side, blocks)],
            send_sem=halo_send.at[kind, side],
            recv_sem=halo_recv.at[kind, side],
            device_id={"space": left if side else right},
            device_id_type=MESH,
        )

    def out_copy(c):
        cut = pl.ds(pl.multiple_of(c * CHUNK, CHUNK), CHUNK)
        return pltpu.make_async_copy(out_v.at[:, cut], out_hbm.at[:, cut], out_sem.at[c])

    barrier = pltpu.get_barrier_semaphore()

    @pl.loop(1, clip)
    def _(p):
        pl.semaphore_signal(
            barrier, inc=1, device_id={"frame": base + peer_of(p)}, device_id_type=MESH
        )

    for side in (left, right):
        pl.semaphore_signal(barrier, inc=1, device_id={"space": side}, device_id_type=MESH)
    lat_in.start()
    wqkv_in.start()

    @pl.loop(0, chunks)
    def _(c):
        own_copy(c).start()

    pl.semaphore_wait(barrier, clip + 1)

    @pl.loop(0, chunks)
    def _(c):
        @pl.loop(1, clip)
        def _(p):
            lat_copy(c, peer_of(p), rank).start()

    wout_in.start()
    lat_in.wait()

    @pl.loop(0, clip)
    def _(i):
        mod[pl.ds(pl.multiple_of(i * per, per), per), :] = modulate(lat[i], cond_ref)

    for b in range(blocks):
        cut = slice(b * block_len, (b + 1) * block_len)
        spots = lax.broadcasted_iota(jnp.int32, (tokens, block_len), 0)
        one_hot = jnp.where(spots == slot_ref[b : b + 1, :], 1.0, 0.0).astype(BF16)
        place[:, cut] = one_hot
        ranked[cut, :] = lax.dot_general(
            one_hot, mod[...], (((0,), (0,)), ((), ())), preferred_element_type=F32
        ).astype(BF16)

    wqkv_in.wait()
    for kind, win in enumerate((kwin, vwin)):
        for lo in range(0, half, 256):
            at = (kind + 1) * width + lo
            part = dot(ranked[...], wqkv[:, at : at + 256]).astype(BF16)
            win[blocks : 2 * blocks, :, lo : lo + 256] = part.reshape(blocks, block_len, 256)
        for side in range(2):
            halo_copy(win, kind, side).start()
    for lo in range(0, half, 256):
        part = dot(ranked[...], wqkv[:, lo : lo + 256]).astype(BF16)
        query[:, :, lo : lo + 256] = part.reshape(blocks, block_len, 256)

    same = lax.rem(lax.broadcasted_iota(jnp.int32, (rows, rows), 0), CHUNK) == lax.rem(
        lax.broadcasted_iota(jnp.int32, (rows, rows), 1), CHUNK
    )

    @pl.loop(0, chunks)
    def _(c):
        own_copy(c).wait()

        @pl.loop(1, clip)
        def _(p):
            lat_copy(c, peer_of(p), peer_of(p)).wait_recv()

        normed = modulate(grp[c].reshape(rows, width), cond_ref)
        q = dot(normed, wqkv[:, half:width]).astype(BF16)
        k = dot(normed, wqkv[:, width + half : 2 * width]).astype(BF16)
        v = dot(normed, wqkv[:, 2 * width + half :]).astype(BF16)
        outs = []
        for h in range(sheads):
            cut = slice(h * head_dim, (h + 1) * head_dim)
            scores = jnp.where(same, dot_t(q[:, cut], k[:, cut]) * scale, -jnp.inf)
            expo = jnp.exp(scores - jnp.max(scores, axis=-1, keepdims=True))
            total = jnp.sum(expo, axis=-1, keepdims=True)
            outs.append((dot(expo.astype(BF16), v[:, cut]) / total).astype(BF16))
        result = jnp.concatenate(outs, axis=1).reshape(clip, CHUNK, half)
        t_out[c] = result
        tmp[c, rank] = t_out[c, rank]

        @pl.loop(1, clip)
        def _(p):
            ret_copy(c, peer_of(p), rank).start()

    for kind, win in enumerate((kwin, vwin)):
        for side in range(2):
            halo_copy(win, kind, side).wait_recv()
    first_block = (me_s - 1) * blocks
    total_blocks = blocks * space_total

    @pl.loop(0, blocks)
    def _(b):
        ids = []
        for n in range(MAXNB):
            at = nb_ref[b, n] - first_block
            at = jnp.where(at >= total_blocks, at - total_blocks, at)
            at = jnp.where(at < 0, at + total_blocks, at)
            ids.append(jnp.clip(at, 0, 3 * blocks - 1))
        keys = [kwin[at] for at in ids]
        vals = [vwin[at] for at in ids]
        q = query[b]
        outs = []
        for h in range(sheads):
            cut = slice(h * head_dim, (h + 1) * head_dim)
            parts = []
            for n in range(MAXNB):
                part = dot_t(q[:, cut], keys[n][:, cut]) * scale
                if n > 0:
                    part = jnp.where(n < cnt_ref[b], part, -jnp.inf)
                parts.append(part)
            scores = jnp.concatenate(parts, axis=1)
            expo = jnp.exp(scores - jnp.max(scores, axis=-1, keepdims=True))
            total = jnp.sum(expo, axis=-1, keepdims=True)
            val = jnp.concatenate([vals[n][:, cut] for n in range(MAXNB)], axis=0)
            outs.append((dot(expo.astype(BF16), val) / total).astype(BF16))
        block_out[pl.ds(pl.multiple_of(b * block_len, block_len), block_len), :] = (
            jnp.concatenate(outs, axis=1)
        )

    spatial = dot(place[...], block_out[...]).astype(BF16)
    wout_in.wait()
    for lo in range(0, width, 256):
        part = dot(spatial, wout[:half, lo : lo + 256])
        sp_mixed[:, :, lo : lo + 256] = part.reshape(clip, per, 256)

    @pl.loop(0, chunks)
    def _(c):
        @pl.loop(1, clip)
        def _(p):
            ret_copy(c, peer_of(p), peer_of(p)).wait_recv()

        cut = pl.ds(pl.multiple_of(c * CHUNK, CHUNK), CHUNK)
        mixed = dot(tmp[c].reshape(rows, half), wout[half:, :]).reshape(clip, CHUNK, width)
        mixed = mixed + sp_mixed[:, cut, :]
        gate = cond_ref[2:3, :].reshape(1, 1, width)
        out_v[:, cut, :] = (lat[:, cut, :].astype(F32) + gate * mixed).astype(BF16)
        out_copy(c).start()

    @pl.loop(0, chunks)
    def _(c):
        out_copy(c).wait()

        @pl.loop(1, clip)
        def _(p):
            lat_copy(c, peer_of(p), rank).wait_send()
            ret_copy(c, peer_of(p), rank).wait_send()

    for kind, win in enumerate((kwin, vwin)):
        for side in range(2):
            halo_copy(win, kind, side).wait_send()


def body(latent, cond, w_qkv, w_out, slot, neighbours, counts):
    tokens, width = latent.shape[1], latent.shape[2]
    blocks = neighbours.shape[0]
    block_len = tokens // blocks
    half = width // 2
    clip = min(8, lax.axis_size("frame"))
    per = tokens // clip
    chunks = per // CHUNK
    vmem = pl.BlockSpec(memory_space=pltpu.VMEM)
    smem = pl.BlockSpec(memory_space=pltpu.SMEM)
    hbm = pl.BlockSpec(memory_space=pl.ANY)
    dma = pltpu.SemaphoreType.DMA
    out = pl.pallas_call(
        functools.partial(kernel, clip),
        out_shape=jax.ShapeDtypeStruct((clip, per, width), BF16),
        in_specs=[hbm, vmem, hbm, hbm, vmem, smem, smem],
        out_specs=hbm,
        scratch_shapes=[
            pltpu.VMEM((clip, per, width), BF16),
            pltpu.VMEM(w_qkv.shape, BF16),
            pltpu.VMEM(w_out.shape, BF16),
            pltpu.VMEM((chunks, clip, CHUNK, width), BF16),
            pltpu.VMEM((tokens, width), BF16),
            pltpu.VMEM((tokens, width), BF16),
            pltpu.VMEM((blocks, block_len, half), BF16),
            pltpu.VMEM((3 * blocks, block_len, half), BF16),
            pltpu.VMEM((3 * blocks, block_len, half), BF16),
            pltpu.VMEM((tokens, tokens), BF16),
            pltpu.VMEM((tokens, half), BF16),
            pltpu.VMEM((clip, per, width), F32),
            pltpu.VMEM((chunks, clip, CHUNK, half), BF16),
            pltpu.VMEM((chunks, clip, CHUNK, half), BF16),
            pltpu.VMEM((clip, per, width), BF16),
            dma((3,)),
            dma((chunks,)),
            dma((chunks, clip)),
            dma((chunks, clip)),
            dma((2, 2)),
            dma((2, 2)),
            dma((chunks, clip)),
            dma((chunks, clip)),
            dma((chunks,)),
        ],
        compiler_params=pltpu.CompilerParams(
            collective_id=0, has_side_effects=True, vmem_limit_bytes=48 * 1024 * 1024
        ),
        cost_estimate=pl.CostEstimate(
            flops=5_000_000_000, bytes_accessed=12_000_000, transcendentals=2_000_000
        ),
    )(
        latent.reshape(clip, per, width),
        cond,
        w_qkv,
        w_out,
        slot.reshape(blocks, block_len),
        neighbours,
        counts,
    )
    return out.reshape(1, tokens, width)


def solution(mesh):
    in_specs = (P("frame", "space", None), P(), P(), P(), P("space"), P("space", None), P("space"))
    out_specs = P("frame", "space", None)
    return jax.shard_map(body, mesh=mesh, in_specs=in_specs, out_specs=out_specs, check_vma=False)
```

```python
import functools
import math

import jax
import jax.numpy as jnp
from jax import lax
from jax.experimental import pallas as pl
from jax.experimental.pallas import tpu as pltpu
from jax.sharding import PartitionSpec as P

HEADS = 8
MAXNB = 4
MESH = pl.DeviceIdType.MESH
F32 = jnp.float32
BF16 = jnp.bfloat16
CHUNK = 16


def modulate(rows, cond_ref):
    rows = rows.astype(F32)
    centred = rows - jnp.mean(rows, axis=-1, keepdims=True)
    normed = centred * lax.rsqrt(jnp.mean(centred * centred, axis=-1, keepdims=True) + 1e-06)
    return (normed * (1.0 + cond_ref[1:2, :]) + cond_ref[0:1, :]).astype(BF16)


def dot(a, b):
    return jnp.dot(a, b, preferred_element_type=F32)


def dot_t(a, b):
    return lax.dot_general(a, b, (((1,), (1,)), ((), ())), preferred_element_type=F32)


def kernel(
    clip,
    lat_hbm,
    cond_hbm,
    wqkv_hbm,
    wout_hbm,
    slot_hbm,
    nb_hbm,
    cnt_hbm,
    out_hbm,
    cond_ref,
    slot_ref,
    nb_ref,
    cnt_ref,
    lat,
    wqkv,
    wout,
    grp,
    mod,
    ranked,
    query,
    kwin,
    vwin,
    place,
    block_out,
    sp_mixed,
    t_out,
    tmp,
    out_v,
    local_sem,
    own_sem,
    lat_send,
    lat_recv,
    halo_send,
    halo_recv,
    ret_send,
    ret_recv,
    out_sem,
):
    space_total = lax.axis_size("space")
    me_s = lax.axis_index("space")
    me_f = lax.axis_index("frame")
    rank = lax.rem(me_f, clip)
    base = me_f - rank
    left = lax.rem(me_s + space_total - 1, space_total)
    right = lax.rem(me_s + 1, space_total)
    per, width = lat.shape[1], lat.shape[2]
    tokens = clip * per
    half = width // 2
    head_dim = width // HEADS
    sheads = HEADS // 2
    blocks, block_len = slot_ref.shape
    chunks = per // CHUNK
    rows = clip * CHUNK
    scale = math.log2(math.e) / math.sqrt(head_dim)

    far_first = sorted(range(1, clip), key=lambda p: abs(2 * p - clip))

    def peer_of(p):
        return lax.rem(rank + p, clip)

    lat_in = pltpu.make_async_copy(lat_hbm, lat, local_sem.at[0])
    wqkv_in = pltpu.make_async_copy(wqkv_hbm, wqkv, local_sem.at[1])
    wout_in = pltpu.make_async_copy(wout_hbm, wout, local_sem.at[2])
    small_in = [
        pltpu.make_async_copy(cond_hbm, cond_ref, local_sem.at[3]),
        pltpu.make_async_copy(slot_hbm, slot_ref, local_sem.at[4]),
        pltpu.make_async_copy(nb_hbm, nb_ref, local_sem.at[5]),
        pltpu.make_async_copy(cnt_hbm, cnt_ref, local_sem.at[6]),
    ]

    def own_copy(c):
        return pltpu.make_async_copy(
            lat_hbm.at[rank, pl.ds(pl.multiple_of(c * CHUNK, CHUNK), CHUNK)],
            grp.at[c, rank],
            own_sem.at[c],
        )

    def lat_copy(c, peer, slot):
        return pltpu.make_async_remote_copy(
            src_ref=lat_hbm.at[peer, pl.ds(pl.multiple_of(c * CHUNK, CHUNK), CHUNK)],
            dst_ref=grp.at[c, slot],
            send_sem=lat_send.at[c, peer],
            recv_sem=lat_recv.at[c, slot],
            device_id={"frame": base + peer},
            device_id_type=MESH,
        )

    def ret_copy(c, peer, slot):
        return pltpu.make_async_remote_copy(
            src_ref=t_out.at[c, peer],
            dst_ref=tmp.at[c, slot],
            send_sem=ret_send.at[c, peer],
            recv_sem=ret_recv.at[c, slot],
            device_id={"frame": base + peer},
            device_id_type=MESH,
        )

    def halo_copy(win, kind, side):
        return pltpu.make_async_remote_copy(
            src_ref=win.at[pl.ds(blocks, blocks)],
            dst_ref=win.at[pl.ds(2 * blocks * side, blocks)],
            send_sem=halo_send.at[kind, side],
            recv_sem=halo_recv.at[kind, side],
            device_id={"space": left if side else right},
            device_id_type=MESH,
        )

    def out_copy(c):
        cut = pl.ds(pl.multiple_of(c * CHUNK, CHUNK), CHUNK)
        return pltpu.make_async_copy(out_v.at[:, cut], out_hbm.at[:, cut], out_sem.at[c])

    barrier = pltpu.get_barrier_semaphore()

    @pl.loop(1, clip)
    def _(p):
        pl.semaphore_signal(
            barrier, inc=1, device_id={"frame": base + peer_of(p)}, device_id_type=MESH
        )

    for side in (left, right):
        pl.semaphore_signal(barrier, inc=1, device_id={"space": side}, device_id_type=MESH)
    lat_in.start()
    for copy in small_in:
        copy.start()
    wqkv_in.start()

    @pl.loop(0, chunks)
    def _(c):
        own_copy(c).start()

    pl.semaphore_wait(barrier, clip + 1)

    @pl.loop(0, chunks)
    def _(c):
        for p in far_first:
            lat_copy(c, peer_of(p), rank).start()

    wout_in.start()
    for copy in small_in:
        copy.wait()
    lat_in.wait()

    @pl.loop(0, clip)
    def _(i):
        mod[pl.ds(pl.multiple_of(i * per, per), per), :] = modulate(lat[i], cond_ref)

    for b in range(blocks):
        cut = slice(b * block_len, (b + 1) * block_len)
        spots = lax.broadcasted_iota(jnp.int32, (tokens, block_len), 0)
        one_hot = jnp.where(spots == slot_ref[b : b + 1, :], 1.0, 0.0).astype(BF16)
        place[:, cut] = one_hot
        ranked[cut, :] = lax.dot_general(
            one_hot, mod[...], (((0,), (0,)), ((), ())), preferred_element_type=F32
        ).astype(BF16)

    wqkv_in.wait()
    for kind, win in enumerate((kwin, vwin)):
        for lo in range(0, half, 256):
            at = (kind + 1) * width + lo
            part = dot(ranked[...], wqkv[:, at : at + 256]).astype(BF16)
            win[blocks : 2 * blocks, :, lo : lo + 256] = part.reshape(blocks, block_len, 256)
        for side in range(2):
            halo_copy(win, kind, side).start()
    for lo in range(0, half, 256):
        part = dot(ranked[...], wqkv[:, lo : lo + 256]).astype(BF16)
        query[:, :, lo : lo + 256] = part.reshape(blocks, block_len, 256)

    same = lax.rem(lax.broadcasted_iota(jnp.int32, (rows, rows), 0), CHUNK) == lax.rem(
        lax.broadcasted_iota(jnp.int32, (rows, rows), 1), CHUNK
    )

    @pl.loop(0, chunks)
    def _(c):
        own_copy(c).wait()

        @pl.loop(1, clip)
        def _(p):
            lat_copy(c, peer_of(p), peer_of(p)).wait_recv()

        normed = modulate(grp[c].reshape(rows, width), cond_ref)
        q = dot(normed, wqkv[:, half:width]).astype(BF16)
        k = dot(normed, wqkv[:, width + half : 2 * width]).astype(BF16)
        v = dot(normed, wqkv[:, 2 * width + half :]).astype(BF16)
        outs = []
        for h in range(sheads):
            cut = slice(h * head_dim, (h + 1) * head_dim)
            scores = jnp.where(same, dot_t(q[:, cut], k[:, cut]), -jnp.inf)
            expo = jnp.exp2((scores - jnp.max(scores, axis=-1, keepdims=True)) * scale)
            total = jnp.sum(expo, axis=-1, keepdims=True)
            outs.append((dot(expo.astype(BF16), v[:, cut]) / total).astype(BF16))
        result = jnp.concatenate(outs, axis=1).reshape(clip, CHUNK, half)
        t_out[c] = result
        tmp[c, rank] = t_out[c, rank]

        for p in far_first:
            ret_copy(c, peer_of(p), rank).start()

    for kind, win in enumerate((kwin, vwin)):
        for side in range(2):
            halo_copy(win, kind, side).wait_recv()
    first_block = (me_s - 1) * blocks
    total_blocks = blocks * space_total

    @pl.loop(0, blocks)
    def _(b):
        ids = []
        for n in range(MAXNB):
            at = nb_ref[b, n] - first_block
            at = jnp.where(at >= total_blocks, at - total_blocks, at)
            at = jnp.where(at < 0, at + total_blocks, at)
            ids.append(jnp.clip(at, 0, 3 * blocks - 1))
        keys = [kwin[at] for at in ids]
        vals = [vwin[at] for at in ids]
        q = query[b]
        outs = []
        for h in range(sheads):
            cut = slice(h * head_dim, (h + 1) * head_dim)
            parts = []
            for n in range(MAXNB):
                part = dot_t(q[:, cut], keys[n][:, cut])
                if n > 0:
                    part = jnp.where(n < cnt_ref[b], part, -jnp.inf)
                parts.append(part)
            scores = jnp.concatenate(parts, axis=1)
            expo = jnp.exp2((scores - jnp.max(scores, axis=-1, keepdims=True)) * scale)
            total = jnp.sum(expo, axis=-1, keepdims=True)
            val = jnp.concatenate([vals[n][:, cut] for n in range(MAXNB)], axis=0)
            outs.append((dot(expo.astype(BF16), val) / total).astype(BF16))
        block_out[pl.ds(pl.multiple_of(b * block_len, block_len), block_len), :] = (
            jnp.concatenate(outs, axis=1)
        )

    spatial = dot(place[...], block_out[...]).astype(BF16)
    wout_in.wait()
    for lo in range(0, width, 256):
        part = dot(spatial, wout[:half, lo : lo + 256])
        sp_mixed[:, :, lo : lo + 256] = part.reshape(clip, per, 256)

    @pl.loop(0, chunks)
    def _(c):
        @pl.loop(1, clip)
        def _(p):
            ret_copy(c, peer_of(p), peer_of(p)).wait_recv()

        cut = pl.ds(pl.multiple_of(c * CHUNK, CHUNK), CHUNK)
        mixed = dot(tmp[c].reshape(rows, half), wout[half:, :]).reshape(clip, CHUNK, width)
        mixed = mixed + sp_mixed[:, cut, :]
        gate = cond_ref[2:3, :].reshape(1, 1, width)
        out_v[:, cut, :] = (lat[:, cut, :].astype(F32) + gate * mixed).astype(BF16)
        out_copy(c).start()

    @pl.loop(0, chunks)
    def _(c):
        out_copy(c).wait()

        @pl.loop(1, clip)
        def _(p):
            lat_copy(c, peer_of(p), rank).wait_send()
            ret_copy(c, peer_of(p), rank).wait_send()

    for kind, win in enumerate((kwin, vwin)):
        for side in range(2):
            halo_copy(win, kind, side).wait_send()


def body(latent, cond, w_qkv, w_out, slot, neighbours, counts):
    tokens, width = latent.shape[1], latent.shape[2]
    blocks = neighbours.shape[0]
    block_len = tokens // blocks
    half = width // 2
    clip = min(8, lax.axis_size("frame"))
    per = tokens // clip
    chunks = per // CHUNK
    hbm = pl.BlockSpec(memory_space=pltpu.HBM)
    dma = pltpu.SemaphoreType.DMA
    out = pl.pallas_call(
        functools.partial(kernel, clip),
        out_shape=jax.ShapeDtypeStruct((clip, per, width), BF16),
        in_specs=[hbm] * 7,
        out_specs=hbm,
        scratch_shapes=[
            pltpu.VMEM(cond.shape, F32),
            pltpu.VMEM((blocks, block_len), jnp.int32),
            pltpu.SMEM(neighbours.shape, jnp.int32),
            pltpu.SMEM(counts.shape, jnp.int32),
            pltpu.VMEM((clip, per, width), BF16),
            pltpu.VMEM(w_qkv.shape, BF16),
            pltpu.VMEM(w_out.shape, BF16),
            pltpu.VMEM((chunks, clip, CHUNK, width), BF16),
            pltpu.VMEM((tokens, width), BF16),
            pltpu.VMEM((tokens, width), BF16),
            pltpu.VMEM((blocks, block_len, half), BF16),
            pltpu.VMEM((3 * blocks, block_len, half), BF16),
            pltpu.VMEM((3 * blocks, block_len, half), BF16),
            pltpu.VMEM((tokens, tokens), BF16),
            pltpu.VMEM((tokens, half), BF16),
            pltpu.VMEM((clip, per, width), F32),
            pltpu.VMEM((chunks, clip, CHUNK, half), BF16),
            pltpu.VMEM((chunks, clip, CHUNK, half), BF16),
            pltpu.VMEM((clip, per, width), BF16),
            dma((7,)),
            dma((chunks,)),
            dma((chunks, clip)),
            dma((chunks, clip)),
            dma((2, 2)),
            dma((2, 2)),
            dma((chunks, clip)),
            dma((chunks, clip)),
            dma((chunks,)),
        ],
        compiler_params=pltpu.CompilerParams(
            collective_id=0, has_side_effects=True, vmem_limit_bytes=48 * 1024 * 1024
        ),
        cost_estimate=pl.CostEstimate(
            flops=5_000_000_000, bytes_accessed=12_000_000, transcendentals=2_000_000
        ),
    )(
        *(
            pltpu.with_memory_space_constraint(x, pltpu.HBM)
            for x in (
                latent.reshape(clip, per, width),
                cond,
                w_qkv,
                w_out,
                slot.reshape(blocks, block_len),
                neighbours,
                counts,
            )
        )
    )
    return out.reshape(1, tokens, width)


def solution(mesh):
    in_specs = (P("frame", "space", None), P(), P(), P(), P("space"), P("space", None), P("space"))
    out_specs = P("frame", "space", None)
    return jax.shard_map(body, mesh=mesh, in_specs=in_specs, out_specs=out_specs, check_vma=False)
```

```python
import functools
import math

import jax
import jax.numpy as jnp
from jax import lax
from jax.experimental import pallas as pl
from jax.experimental.pallas import tpu as pltpu
from jax.sharding import PartitionSpec as P

HEADS = 8
MAXNB = 4
MESH = pl.DeviceIdType.MESH
F32 = jnp.float32
BF16 = jnp.bfloat16
CHUNK = 16


def modulate(rows, cond_ref):
    rows = rows.astype(F32)
    centred = rows - jnp.mean(rows, axis=-1, keepdims=True)
    normed = centred * lax.rsqrt(jnp.mean(centred * centred, axis=-1, keepdims=True) + 1e-06)
    return (normed * (1.0 + cond_ref[1:2, :]) + cond_ref[0:1, :]).astype(BF16)


def dot(a, b):
    return jnp.dot(a, b, preferred_element_type=F32)


def dot_t(a, b):
    return lax.dot_general(a, b, (((1,), (1,)), ((), ())), preferred_element_type=F32)


def kernel(
    clip,
    lat_hbm,
    cond_hbm,
    wqkv_hbm,
    wout_hbm,
    slot_hbm,
    nb_hbm,
    cnt_hbm,
    out_hbm,
    cond_ref,
    slot_ref,
    nb_ref,
    cnt_ref,
    lat,
    wqkv,
    wout,
    grp,
    mod,
    ranked,
    query,
    kwin,
    vwin,
    place,
    block_out,
    sp_mixed,
    t_out,
    tmp,
    out_v,
    local_sem,
    own_sem,
    lat_send,
    lat_recv,
    halo_send,
    halo_recv,
    ret_send,
    ret_recv,
    out_sem,
):
    space_total = lax.axis_size("space")
    me_s = lax.axis_index("space")
    me_f = lax.axis_index("frame")
    rank = lax.rem(me_f, clip)
    base = me_f - rank
    left = lax.rem(me_s + space_total - 1, space_total)
    right = lax.rem(me_s + 1, space_total)
    per, width = lat.shape[1], lat.shape[2]
    tokens = clip * per
    half = width // 2
    head_dim = width // HEADS
    sheads = HEADS // 2
    blocks, block_len = slot_ref.shape
    chunks = per // CHUNK
    rows = clip * CHUNK
    scale = math.log2(math.e) / math.sqrt(head_dim)

    far_first = sorted(range(1, clip), key=lambda p: abs(2 * p - clip))

    def peer_of(p):
        return lax.rem(rank + p, clip)

    lat_in = pltpu.make_async_copy(lat_hbm, lat, local_sem.at[0])
    wqkv_in = pltpu.make_async_copy(wqkv_hbm, wqkv, local_sem.at[1])
    wout_in = pltpu.make_async_copy(wout_hbm, wout, local_sem.at[2])
    small_in = [
        pltpu.make_async_copy(cond_hbm, cond_ref, local_sem.at[3]),
        pltpu.make_async_copy(slot_hbm, slot_ref, local_sem.at[4]),
        pltpu.make_async_copy(nb_hbm, nb_ref, local_sem.at[5]),
        pltpu.make_async_copy(cnt_hbm, cnt_ref, local_sem.at[6]),
    ]

    def own_copy(c):
        return pltpu.make_async_copy(
            lat_hbm.at[rank, pl.ds(pl.multiple_of(c * CHUNK, CHUNK), CHUNK)],
            grp.at[c, rank],
            own_sem.at[c],
        )

    def lat_copy(c, peer, slot):
        return pltpu.make_async_remote_copy(
            src_ref=lat_hbm.at[peer, pl.ds(pl.multiple_of(c * CHUNK, CHUNK), CHUNK)],
            dst_ref=grp.at[c, slot],
            send_sem=lat_send.at[c, peer],
            recv_sem=lat_recv.at[c, slot],
            device_id={"frame": base + peer},
            device_id_type=MESH,
        )

    def ret_copy(c, peer, slot):
        return pltpu.make_async_remote_copy(
            src_ref=t_out.at[c, peer],
            dst_ref=tmp.at[c, slot],
            send_sem=ret_send.at[c, peer],
            recv_sem=ret_recv.at[c, slot],
            device_id={"frame": base + peer},
            device_id_type=MESH,
        )

    def halo_copy(win, kind, part, side):
        at = part * (blocks // 2)
        return pltpu.make_async_remote_copy(
            src_ref=win.at[pl.ds(blocks + at, blocks // 2)],
            dst_ref=win.at[pl.ds(2 * blocks * side + at, blocks // 2)],
            send_sem=halo_send.at[kind, part, side],
            recv_sem=halo_recv.at[kind, part, side],
            device_id={"space": left if side else right},
            device_id_type=MESH,
        )

    def out_copy(c):
        cut = pl.ds(pl.multiple_of(c * CHUNK, CHUNK), CHUNK)
        return pltpu.make_async_copy(out_v.at[:, cut], out_hbm.at[:, cut], out_sem.at[c])

    barrier = pltpu.get_barrier_semaphore()

    @pl.loop(1, clip)
    def _(p):
        pl.semaphore_signal(
            barrier, inc=1, device_id={"frame": base + peer_of(p)}, device_id_type=MESH
        )

    for side in (left, right):
        pl.semaphore_signal(barrier, inc=1, device_id={"space": side}, device_id_type=MESH)
    lat_in.start()
    for copy in small_in:
        copy.start()
    wqkv_in.start()

    @pl.loop(0, chunks)
    def _(c):
        own_copy(c).start()

    pl.semaphore_wait(barrier, clip + 1)

    def send_latent(c):
        for p in far_first:
            lat_copy(c, peer_of(p), rank).start()

    send_latent(0)

    wout_in.start()
    for copy in small_in:
        copy.wait()
    lat_in.wait()

    @pl.loop(0, clip)
    def _(i):
        mod[pl.ds(pl.multiple_of(i * per, per), per), :] = modulate(lat[i], cond_ref)

    for b in range(blocks):
        cut = slice(b * block_len, (b + 1) * block_len)
        spots = lax.broadcasted_iota(jnp.int32, (tokens, block_len), 0)
        one_hot = jnp.where(spots == slot_ref[b : b + 1, :], 1.0, 0.0).astype(BF16)
        place[:, cut] = one_hot
        ranked[cut, :] = lax.dot_general(
            one_hot, mod[...], (((0,), (0,)), ((), ())), preferred_element_type=F32
        ).astype(BF16)

    wqkv_in.wait()
    for kind, win in enumerate((kwin, vwin)):
        for lo in range(0, half, 256):
            at = (kind + 1) * width + lo
            part = dot(ranked[...], wqkv[:, at : at + 256]).astype(BF16)
            win[blocks : 2 * blocks, :, lo : lo + 256] = part.reshape(blocks, block_len, 256)
        for part in range(2):
            for side in range(2):
                halo_copy(win, kind, part, side).start()
            step = 2 * kind + part + 1
            if step < chunks:
                send_latent(step)
    for c in range(5, chunks):
        send_latent(c)
    for lo in range(0, half, 256):
        part = dot(ranked[...], wqkv[:, lo : lo + 256]).astype(BF16)
        query[:, :, lo : lo + 256] = part.reshape(blocks, block_len, 256)

    same = lax.rem(lax.broadcasted_iota(jnp.int32, (rows, rows), 0), CHUNK) == lax.rem(
        lax.broadcasted_iota(jnp.int32, (rows, rows), 1), CHUNK
    )

    @pl.loop(0, chunks)
    def _(c):
        own_copy(c).wait()

        @pl.loop(1, clip)
        def _(p):
            lat_copy(c, peer_of(p), peer_of(p)).wait_recv()

        normed = modulate(grp[c].reshape(rows, width), cond_ref)
        q = dot(normed, wqkv[:, half:width]).astype(BF16)
        k = dot(normed, wqkv[:, width + half : 2 * width]).astype(BF16)
        v = dot(normed, wqkv[:, 2 * width + half :]).astype(BF16)
        outs = []
        for h in range(sheads):
            cut = slice(h * head_dim, (h + 1) * head_dim)
            scores = jnp.where(same, dot_t(q[:, cut], k[:, cut]), -jnp.inf)
            expo = jnp.exp2((scores - jnp.max(scores, axis=-1, keepdims=True)) * scale)
            total = jnp.sum(expo, axis=-1, keepdims=True)
            outs.append((dot(expo.astype(BF16), v[:, cut]) / total).astype(BF16))
        result = jnp.concatenate(outs, axis=1).reshape(clip, CHUNK, half)
        t_out[c] = result
        tmp[c, rank] = t_out[c, rank]

        for p in far_first:
            ret_copy(c, peer_of(p), rank).start()

    for kind, win in enumerate((kwin, vwin)):
        for part in range(2):
            for side in range(2):
                halo_copy(win, kind, part, side).wait_recv()
    first_block = (me_s - 1) * blocks
    total_blocks = blocks * space_total

    @pl.loop(0, blocks)
    def _(b):
        ids = []
        for n in range(MAXNB):
            at = nb_ref[b, n] - first_block
            at = jnp.where(at >= total_blocks, at - total_blocks, at)
            at = jnp.where(at < 0, at + total_blocks, at)
            ids.append(jnp.clip(at, 0, 3 * blocks - 1))
        keys = [kwin[at] for at in ids]
        vals = [vwin[at] for at in ids]
        q = query[b]
        outs = []
        for h in range(sheads):
            cut = slice(h * head_dim, (h + 1) * head_dim)
            parts = []
            for n in range(MAXNB):
                part = dot_t(q[:, cut], keys[n][:, cut])
                if n > 0:
                    part = jnp.where(n < cnt_ref[b], part, -jnp.inf)
                parts.append(part)
            scores = jnp.concatenate(parts, axis=1)
            expo = jnp.exp2((scores - jnp.max(scores, axis=-1, keepdims=True)) * scale)
            total = jnp.sum(expo, axis=-1, keepdims=True)
            val = jnp.concatenate([vals[n][:, cut] for n in range(MAXNB)], axis=0)
            outs.append((dot(expo.astype(BF16), val) / total).astype(BF16))
        block_out[pl.ds(pl.multiple_of(b * block_len, block_len), block_len), :] = (
            jnp.concatenate(outs, axis=1)
        )

    spatial = dot(place[...], block_out[...]).astype(BF16)
    wout_in.wait()
    for lo in range(0, width, 256):
        part = dot(spatial, wout[:half, lo : lo + 256])
        sp_mixed[:, :, lo : lo + 256] = part.reshape(clip, per, 256)

    @pl.loop(0, chunks)
    def _(c):
        @pl.loop(1, clip)
        def _(p):
            ret_copy(c, peer_of(p), peer_of(p)).wait_recv()

        cut = pl.ds(pl.multiple_of(c * CHUNK, CHUNK), CHUNK)
        mixed = dot(tmp[c].reshape(rows, half), wout[half:, :]).reshape(clip, CHUNK, width)
        mixed = mixed + sp_mixed[:, cut, :]
        gate = cond_ref[2:3, :].reshape(1, 1, width)
        out_v[:, cut, :] = (lat[:, cut, :].astype(F32) + gate * mixed).astype(BF16)
        out_copy(c).start()

    @pl.loop(0, chunks)
    def _(c):
        out_copy(c).wait()

        @pl.loop(1, clip)
        def _(p):
            lat_copy(c, peer_of(p), rank).wait_send()
            ret_copy(c, peer_of(p), rank).wait_send()

    for kind, win in enumerate((kwin, vwin)):
        for part in range(2):
            for side in range(2):
                halo_copy(win, kind, part, side).wait_send()


def body(latent, cond, w_qkv, w_out, slot, neighbours, counts):
    tokens, width = latent.shape[1], latent.shape[2]
    blocks = neighbours.shape[0]
    block_len = tokens // blocks
    half = width // 2
    clip = min(8, lax.axis_size("frame"))
    per = tokens // clip
    chunks = per // CHUNK
    hbm = pl.BlockSpec(memory_space=pltpu.HBM)
    dma = pltpu.SemaphoreType.DMA
    out = pl.pallas_call(
        functools.partial(kernel, clip),
        out_shape=jax.ShapeDtypeStruct((clip, per, width), BF16),
        in_specs=[hbm] * 7,
        out_specs=hbm,
        scratch_shapes=[
            pltpu.VMEM(cond.shape, F32),
            pltpu.VMEM((blocks, block_len), jnp.int32),
            pltpu.SMEM(neighbours.shape, jnp.int32),
            pltpu.SMEM(counts.shape, jnp.int32),
            pltpu.VMEM((clip, per, width), BF16),
            pltpu.VMEM(w_qkv.shape, BF16),
            pltpu.VMEM(w_out.shape, BF16),
            pltpu.VMEM((chunks, clip, CHUNK, width), BF16),
            pltpu.VMEM((tokens, width), BF16),
            pltpu.VMEM((tokens, width), BF16),
            pltpu.VMEM((blocks, block_len, half), BF16),
            pltpu.VMEM((3 * blocks, block_len, half), BF16),
            pltpu.VMEM((3 * blocks, block_len, half), BF16),
            pltpu.VMEM((tokens, tokens), BF16),
            pltpu.VMEM((tokens, half), BF16),
            pltpu.VMEM((clip, per, width), F32),
            pltpu.VMEM((chunks, clip, CHUNK, half), BF16),
            pltpu.VMEM((chunks, clip, CHUNK, half), BF16),
            pltpu.VMEM((clip, per, width), BF16),
            dma((7,)),
            dma((chunks,)),
            dma((chunks, clip)),
            dma((chunks, clip)),
            dma((2, 2, 2)),
            dma((2, 2, 2)),
            dma((chunks, clip)),
            dma((chunks, clip)),
            dma((chunks,)),
        ],
        compiler_params=pltpu.CompilerParams(
            collective_id=0, has_side_effects=True, vmem_limit_bytes=48 * 1024 * 1024
        ),
        cost_estimate=pl.CostEstimate(
            flops=5_000_000_000, bytes_accessed=12_000_000, transcendentals=2_000_000
        ),
    )(
        *(
            pltpu.with_memory_space_constraint(x, pltpu.HBM)
            for x in (
                latent.reshape(clip, per, width),
                cond,
                w_qkv,
                w_out,
                slot.reshape(blocks, block_len),
                neighbours,
                counts,
            )
        )
    )
    return out.reshape(1, tokens, width)


def solution(mesh):
    in_specs = (P("frame", "space", None), P(), P(), P(), P("space"), P("space", None), P("space"))
    out_specs = P("frame", "space", None)
    return jax.shard_map(body, mesh=mesh, in_specs=in_specs, out_specs=out_specs, check_vma=False)
```

```python
import functools
import math

import jax
import jax.numpy as jnp
from jax import lax
from jax.experimental import pallas as pl
from jax.experimental.pallas import tpu as pltpu
from jax.sharding import PartitionSpec as P

HEADS = 8
MAXNB = 4
MESH = pl.DeviceIdType.MESH
F32 = jnp.float32
BF16 = jnp.bfloat16
CHUNK = 16


def modulate(rows, cond_ref):
    rows = rows.astype(F32)
    centred = rows - jnp.mean(rows, axis=-1, keepdims=True)
    normed = centred * lax.rsqrt(jnp.mean(centred * centred, axis=-1, keepdims=True) + 1e-06)
    return (normed * (1.0 + cond_ref[1:2, :]) + cond_ref[0:1, :]).astype(BF16)


def dot(a, b):
    return jnp.dot(a, b, preferred_element_type=F32)


def dot_t(a, b):
    return lax.dot_general(a, b, (((1,), (1,)), ((), ())), preferred_element_type=F32)


def kernel(
    clip,
    lat_hbm,
    cond_hbm,
    wqkv_hbm,
    wout_hbm,
    slot_hbm,
    nb_hbm,
    cnt_hbm,
    out_hbm,
    cond_ref,
    slot_ref,
    nb_ref,
    cnt_ref,
    lat,
    wqkv,
    wout,
    grp,
    mod,
    ranked,
    query,
    kwin,
    vwin,
    place,
    block_out,
    sp_mixed,
    t_out,
    tmp,
    out_v,
    local_sem,
    w_sem,
    own_sem,
    lat_send,
    lat_recv,
    halo_send,
    halo_recv,
    ret_send,
    ret_recv,
    out_sem,
):
    space_total = lax.axis_size("space")
    me_s = lax.axis_index("space")
    me_f = lax.axis_index("frame")
    rank = lax.rem(me_f, clip)
    base = me_f - rank
    left = lax.rem(me_s + space_total - 1, space_total)
    right = lax.rem(me_s + 1, space_total)
    per, width = lat.shape[1], lat.shape[2]
    tokens = clip * per
    half = width // 2
    head_dim = width // HEADS
    sheads = HEADS // 2
    blocks, block_len = slot_ref.shape
    chunks = per // CHUNK
    rows = clip * CHUNK
    scale = math.log2(math.e) / math.sqrt(head_dim)

    far_first = sorted(range(1, clip), key=lambda p: abs(2 * p - clip))

    def peer_of(p):
        return lax.rem(rank + p, clip)

    lat_in = pltpu.make_async_copy(lat_hbm, lat, local_sem.at[0])
    w_in = []
    for i, at in enumerate((2, 4, 0, 1, 3, 5)):
        cut = pl.ds(at * half, half)
        w_in.append(pltpu.make_async_copy(wqkv_hbm.at[:, cut], wqkv.at[:, cut], w_sem.at[i]))
    wout_in = pltpu.make_async_copy(wout_hbm, wout, local_sem.at[2])
    small_in = [
        pltpu.make_async_copy(cond_hbm, cond_ref, local_sem.at[3]),
        pltpu.make_async_copy(slot_hbm, slot_ref, local_sem.at[4]),
        pltpu.make_async_copy(nb_hbm, nb_ref, local_sem.at[5]),
        pltpu.make_async_copy(cnt_hbm, cnt_ref, local_sem.at[6]),
    ]

    def own_copy(c):
        return pltpu.make_async_copy(
            lat_hbm.at[rank, pl.ds(pl.multiple_of(c * CHUNK, CHUNK), CHUNK)],
            grp.at[c, rank],
            own_sem.at[c],
        )

    def lat_copy(c, peer, slot):
        return pltpu.make_async_remote_copy(
            src_ref=lat_hbm.at[peer, pl.ds(pl.multiple_of(c * CHUNK, CHUNK), CHUNK)],
            dst_ref=grp.at[c, slot],
            send_sem=lat_send.at[c, peer],
            recv_sem=lat_recv.at[c, slot],
            device_id={"frame": base + peer},
            device_id_type=MESH,
        )

    def ret_copy(c, peer, slot):
        return pltpu.make_async_remote_copy(
            src_ref=t_out.at[c, peer],
            dst_ref=tmp.at[c, slot],
            send_sem=ret_send.at[c, peer],
            recv_sem=ret_recv.at[c, slot],
            device_id={"frame": base + peer},
            device_id_type=MESH,
        )

    def halo_copy(win, kind, b, side):
        return pltpu.make_async_remote_copy(
            src_ref=win.at[blocks + b],
            dst_ref=win.at[2 * blocks * side + b],
            send_sem=halo_send.at[kind, side, b],
            recv_sem=halo_recv.at[kind, side, b],
            device_id={"space": left if side else right},
            device_id_type=MESH,
        )

    def out_copy(c):
        cut = pl.ds(pl.multiple_of(c * CHUNK, CHUNK), CHUNK)
        return pltpu.make_async_copy(out_v.at[:, cut], out_hbm.at[:, cut], out_sem.at[c])

    barrier = pltpu.get_barrier_semaphore()

    @pl.loop(1, clip)
    def _(p):
        pl.semaphore_signal(
            barrier, inc=1, device_id={"frame": base + peer_of(p)}, device_id_type=MESH
        )

    for side in (left, right):
        pl.semaphore_signal(barrier, inc=1, device_id={"space": side}, device_id_type=MESH)
    lat_in.start()
    for copy in small_in:
        copy.start()
    for copy in w_in:
        copy.start()

    @pl.loop(0, chunks)
    def _(c):
        own_copy(c).start()

    pl.semaphore_wait(barrier, clip + 1)

    def send_latent(c):
        for p in far_first:
            lat_copy(c, peer_of(p), rank).start()

    send_latent(0)

    wout_in.start()
    for copy in small_in:
        copy.wait()
    lat_in.wait()

    @pl.loop(0, clip)
    def _(i):
        mod[pl.ds(pl.multiple_of(i * per, per), per), :] = modulate(lat[i], cond_ref)

    for b in range(blocks):
        cut = slice(b * block_len, (b + 1) * block_len)
        spots = lax.broadcasted_iota(jnp.int32, (tokens, block_len), 0)
        one_hot = jnp.where(spots == slot_ref[b : b + 1, :], 1.0, 0.0).astype(BF16)
        place[:, cut] = one_hot
        picked = lax.dot_general(
            one_hot, mod[...], (((0,), (0,)), ((), ())), preferred_element_type=F32
        ).astype(BF16)
        ranked[cut, :] = picked
        for kind, win in enumerate((kwin, vwin)):
            if b == 0:
                w_in[kind].wait()
            at = (kind + 1) * width
            win[blocks + b] = dot(picked, wqkv[:, at : at + half]).astype(BF16)
            for side in range(2):
                halo_copy(win, kind, b, side).start()
        if b + 1 < chunks:
            send_latent(b + 1)
    for c in range(blocks + 1, chunks):
        send_latent(c)
    w_in[2].wait()
    for lo in range(0, half, 256):
        part = dot(ranked[...], wqkv[:, lo : lo + 256]).astype(BF16)
        query[:, :, lo : lo + 256] = part.reshape(blocks, block_len, 256)
    for copy in w_in[3:]:
        copy.wait()

    same = lax.rem(lax.broadcasted_iota(jnp.int32, (rows, rows), 0), CHUNK) == lax.rem(
        lax.broadcasted_iota(jnp.int32, (rows, rows), 1), CHUNK
    )

    def temporal(c):
        own_copy(c).wait()

        @pl.loop(1, clip)
        def _(p):
            lat_copy(c, peer_of(p), peer_of(p)).wait_recv()

        normed = modulate(grp[c].reshape(rows, width), cond_ref)
        q = dot(normed, wqkv[:, half:width]).astype(BF16)
        k = dot(normed, wqkv[:, width + half : 2 * width]).astype(BF16)
        v = dot(normed, wqkv[:, 2 * width + half :]).astype(BF16)
        outs = []
        for h in range(sheads):
            cut = slice(h * head_dim, (h + 1) * head_dim)
            scores = jnp.where(same, dot_t(q[:, cut], k[:, cut]), -jnp.inf)
            expo = jnp.exp2((scores - jnp.max(scores, axis=-1, keepdims=True)) * scale)
            total = jnp.sum(expo, axis=-1, keepdims=True)
            outs.append((dot(expo.astype(BF16), v[:, cut]) / total).astype(BF16))
        result = jnp.concatenate(outs, axis=1).reshape(clip, CHUNK, half)
        t_out[c] = result
        tmp[c, rank] = t_out[c, rank]

        for p in far_first:
            ret_copy(c, peer_of(p), rank).start()

    pl.loop(0, chunks - 1)(temporal)

    for kind, win in enumerate((kwin, vwin)):
        for side in range(2):

            @pl.loop(0, blocks)
            def _(b):
                halo_copy(win, kind, b, side).wait_recv()
    first_block = (me_s - 1) * blocks
    total_blocks = blocks * space_total

    @pl.loop(0, blocks)
    def _(b):
        ids = []
        for n in range(MAXNB):
            at = nb_ref[b, n] - first_block
            at = jnp.where(at >= total_blocks, at - total_blocks, at)
            at = jnp.where(at < 0, at + total_blocks, at)
            ids.append(jnp.clip(at, 0, 3 * blocks - 1))
        keys = [kwin[at] for at in ids]
        vals = [vwin[at] for at in ids]
        q = query[b]
        outs = []
        for h in range(sheads):
            cut = slice(h * head_dim, (h + 1) * head_dim)
            parts = []
            for n in range(MAXNB):
                part = dot_t(q[:, cut], keys[n][:, cut])
                if n > 0:
                    part = jnp.where(n < cnt_ref[b], part, -jnp.inf)
                parts.append(part)
            scores = jnp.concatenate(parts, axis=1)
            expo = jnp.exp2((scores - jnp.max(scores, axis=-1, keepdims=True)) * scale)
            total = jnp.sum(expo, axis=-1, keepdims=True)
            val = jnp.concatenate([vals[n][:, cut] for n in range(MAXNB)], axis=0)
            outs.append((dot(expo.astype(BF16), val) / total).astype(BF16))
        block_out[pl.ds(pl.multiple_of(b * block_len, block_len), block_len), :] = (
            jnp.concatenate(outs, axis=1)
        )

    temporal(chunks - 1)
    spatial = dot(place[...], block_out[...]).astype(BF16)
    wout_in.wait()
    for lo in range(0, width, 256):
        part = dot(spatial, wout[:half, lo : lo + 256])
        sp_mixed[:, :, lo : lo + 256] = part.reshape(clip, per, 256)

    @pl.loop(0, chunks)
    def _(c):
        @pl.loop(1, clip)
        def _(p):
            ret_copy(c, peer_of(p), peer_of(p)).wait_recv()

        cut = pl.ds(pl.multiple_of(c * CHUNK, CHUNK), CHUNK)
        mixed = dot(tmp[c].reshape(rows, half), wout[half:, :]).reshape(clip, CHUNK, width)
        mixed = mixed + sp_mixed[:, cut, :]
        gate = cond_ref[2:3, :].reshape(1, 1, width)
        out_v[:, cut, :] = (lat[:, cut, :].astype(F32) + gate * mixed).astype(BF16)
        out_copy(c).start()

    @pl.loop(0, chunks)
    def _(c):
        out_copy(c).wait()

        @pl.loop(1, clip)
        def _(p):
            lat_copy(c, peer_of(p), rank).wait_send()
            ret_copy(c, peer_of(p), rank).wait_send()

    for kind, win in enumerate((kwin, vwin)):
        for side in range(2):

            @pl.loop(0, blocks)
            def _(b):
                halo_copy(win, kind, b, side).wait_send()


def body(latent, cond, w_qkv, w_out, slot, neighbours, counts):
    tokens, width = latent.shape[1], latent.shape[2]
    blocks = neighbours.shape[0]
    block_len = tokens // blocks
    half = width // 2
    clip = min(8, lax.axis_size("frame"))
    per = tokens // clip
    chunks = per // CHUNK
    hbm = pl.BlockSpec(memory_space=pltpu.HBM)
    dma = pltpu.SemaphoreType.DMA
    out = pl.pallas_call(
        functools.partial(kernel, clip),
        out_shape=jax.ShapeDtypeStruct((clip, per, width), BF16),
        in_specs=[hbm] * 7,
        out_specs=hbm,
        scratch_shapes=[
            pltpu.VMEM(cond.shape, F32),
            pltpu.VMEM((blocks, block_len), jnp.int32),
            pltpu.SMEM(neighbours.shape, jnp.int32),
            pltpu.SMEM(counts.shape, jnp.int32),
            pltpu.VMEM((clip, per, width), BF16),
            pltpu.VMEM(w_qkv.shape, BF16),
            pltpu.VMEM(w_out.shape, BF16),
            pltpu.VMEM((chunks, clip, CHUNK, width), BF16),
            pltpu.VMEM((tokens, width), BF16),
            pltpu.VMEM((tokens, width), BF16),
            pltpu.VMEM((blocks, block_len, half), BF16),
            pltpu.VMEM((3 * blocks, block_len, half), BF16),
            pltpu.VMEM((3 * blocks, block_len, half), BF16),
            pltpu.VMEM((tokens, tokens), BF16),
            pltpu.VMEM((tokens, half), BF16),
            pltpu.VMEM((clip, per, width), F32),
            pltpu.VMEM((chunks, clip, CHUNK, half), BF16),
            pltpu.VMEM((chunks, clip, CHUNK, half), BF16),
            pltpu.VMEM((clip, per, width), BF16),
            dma((7,)),
            dma((6,)),
            dma((chunks,)),
            dma((chunks, clip)),
            dma((chunks, clip)),
            dma((2, 2, blocks)),
            dma((2, 2, blocks)),
            dma((chunks, clip)),
            dma((chunks, clip)),
            dma((chunks,)),
        ],
        compiler_params=pltpu.CompilerParams(
            collective_id=0, has_side_effects=True, vmem_limit_bytes=48 * 1024 * 1024
        ),
        cost_estimate=pl.CostEstimate(
            flops=5_000_000_000, bytes_accessed=12_000_000, transcendentals=2_000_000
        ),
    )(
        *(
            pltpu.with_memory_space_constraint(x, pltpu.HBM)
            for x in (
                latent.reshape(clip, per, width),
                cond,
                w_qkv,
                w_out,
                slot.reshape(blocks, block_len),
                neighbours,
                counts,
            )
        )
    )
    return out.reshape(1, tokens, width)


def solution(mesh):
    in_specs = (P("frame", "space", None), P(), P(), P(), P("space"), P("space", None), P("space"))
    out_specs = P("frame", "space", None)
    return jax.shard_map(body, mesh=mesh, in_specs=in_specs, out_specs=out_specs, check_vma=False)
```

```python
import functools
import math

import jax
import jax.numpy as jnp
from jax import lax
from jax.experimental import pallas as pl
from jax.experimental.pallas import tpu as pltpu
from jax.sharding import PartitionSpec as P

HEADS = 8
MAXNB = 4
MESH = pl.DeviceIdType.MESH
F32 = jnp.float32
BF16 = jnp.bfloat16
CHUNK = 16


def modulate(rows, cond_ref):
    rows = rows.astype(F32)
    centred = rows - jnp.mean(rows, axis=-1, keepdims=True)
    normed = centred * lax.rsqrt(jnp.mean(centred * centred, axis=-1, keepdims=True) + 1e-06)
    return (normed * (1.0 + cond_ref[1:2, :]) + cond_ref[0:1, :]).astype(BF16)


def dot(a, b):
    return jnp.dot(a, b, preferred_element_type=F32)


def dot_t(a, b):
    return lax.dot_general(a, b, (((1,), (1,)), ((), ())), preferred_element_type=F32)


def kernel(
    clip,
    lat_hbm,
    cond_hbm,
    wqkv_hbm,
    wout_hbm,
    slot_hbm,
    nb_hbm,
    cnt_hbm,
    out_hbm,
    cond_ref,
    slot_ref,
    nb_ref,
    cnt_ref,
    lat,
    wqkv,
    wout,
    grp,
    mod,
    ranked,
    query,
    kwin,
    vwin,
    place,
    block_out,
    sp_mixed,
    t_out,
    tmp,
    out_v,
    local_sem,
    w_sem,
    own_sem,
    lat_send,
    lat_recv,
    halo_send,
    halo_recv,
    ret_send,
    ret_recv,
    out_sem,
):
    space_total = lax.axis_size("space")
    me_s = lax.axis_index("space")
    me_f = lax.axis_index("frame")
    rank = lax.rem(me_f, clip)
    base = me_f - rank
    left = lax.rem(me_s + space_total - 1, space_total)
    right = lax.rem(me_s + 1, space_total)
    per, width = lat.shape[1], lat.shape[2]
    tokens = clip * per
    half = width // 2
    head_dim = width // HEADS
    sheads = HEADS // 2
    blocks, block_len = slot_ref.shape
    chunks = per // CHUNK
    rows = clip * CHUNK
    scale = math.log2(math.e) / math.sqrt(head_dim)

    far_first = sorted(range(1, clip), key=lambda p: abs(2 * p - clip))

    def peer_of(p):
        return lax.rem(rank + p, clip)

    lat_in = pltpu.make_async_copy(lat_hbm, lat, local_sem.at[0])
    w_in = []
    for i, at in enumerate((2, 4, 0, 1, 3, 5)):
        cut = pl.ds(at * half, half)
        w_in.append(pltpu.make_async_copy(wqkv_hbm.at[:, cut], wqkv.at[:, cut], w_sem.at[i]))
    wout_in = pltpu.make_async_copy(wout_hbm, wout, local_sem.at[2])
    small_in = [
        pltpu.make_async_copy(cond_hbm, cond_ref, local_sem.at[3]),
        pltpu.make_async_copy(slot_hbm, slot_ref, local_sem.at[4]),
        pltpu.make_async_copy(nb_hbm, nb_ref, local_sem.at[5]),
        pltpu.make_async_copy(cnt_hbm, cnt_ref, local_sem.at[6]),
    ]

    def own_copy(c):
        return pltpu.make_async_copy(
            lat_hbm.at[rank, pl.ds(pl.multiple_of(c * CHUNK, CHUNK), CHUNK)],
            grp.at[c, rank],
            own_sem.at[c],
        )

    def lat_copy(c, peer, slot):
        return pltpu.make_async_remote_copy(
            src_ref=lat_hbm.at[peer, pl.ds(pl.multiple_of(c * CHUNK, CHUNK), CHUNK)],
            dst_ref=grp.at[c, slot],
            send_sem=lat_send.at[c, peer],
            recv_sem=lat_recv.at[c, slot],
            device_id={"frame": base + peer},
            device_id_type=MESH,
        )

    def ret_copy(c, peer, slot):
        return pltpu.make_async_remote_copy(
            src_ref=t_out.at[c, peer],
            dst_ref=tmp.at[c, slot],
            send_sem=ret_send.at[c, peer],
            recv_sem=ret_recv.at[c, slot],
            device_id={"frame": base + peer},
            device_id_type=MESH,
        )

    def halo_copy(win, kind, b, side):
        return pltpu.make_async_remote_copy(
            src_ref=win.at[blocks + b],
            dst_ref=win.at[2 * blocks * side + b],
            send_sem=halo_send.at[kind, side, b],
            recv_sem=halo_recv.at[kind, side, b],
            device_id={"space": left if side else right},
            device_id_type=MESH,
        )

    def out_copy(c):
        cut = pl.ds(pl.multiple_of(c * CHUNK, CHUNK), CHUNK)
        return pltpu.make_async_copy(out_v.at[:, cut], out_hbm.at[:, cut], out_sem.at[c])

    barrier = pltpu.get_barrier_semaphore()

    @pl.loop(1, clip)
    def _(p):
        pl.semaphore_signal(
            barrier, inc=1, device_id={"frame": base + peer_of(p)}, device_id_type=MESH
        )

    for side in (left, right):
        pl.semaphore_signal(barrier, inc=1, device_id={"space": side}, device_id_type=MESH)
    lat_in.start()
    for copy in small_in:
        copy.start()
    for copy in w_in:
        copy.start()

    @pl.loop(0, chunks)
    def _(c):
        own_copy(c).start()

    pl.semaphore_wait(barrier, clip + 1)

    def send_latent(c):
        for p in far_first:
            lat_copy(c, peer_of(p), rank).start()

    send_latent(0)

    wout_in.start()
    for copy in small_in:
        copy.wait()
    lat_in.wait()

    @pl.loop(0, clip)
    def _(i):
        mod[pl.ds(pl.multiple_of(i * per, per), per), :] = modulate(lat[i], cond_ref)

    for b in range(blocks):
        cut = slice(b * block_len, (b + 1) * block_len)
        spots = lax.broadcasted_iota(jnp.int32, (tokens, block_len), 0)
        one_hot = jnp.where(spots == slot_ref[b : b + 1, :], 1.0, 0.0).astype(BF16)
        place[:, cut] = one_hot
        picked = lax.dot_general(
            one_hot, mod[...], (((0,), (0,)), ((), ())), preferred_element_type=F32
        ).astype(BF16)
        ranked[cut, :] = picked
        for kind, win in enumerate((kwin, vwin)):
            if b == 0:
                w_in[kind].wait()
            at = (kind + 1) * width
            win[blocks + b] = dot(picked, wqkv[:, at : at + half]).astype(BF16)
            for side in range(2):
                halo_copy(win, kind, b, side).start()
        if b + 1 < chunks:
            send_latent(b + 1)
    for c in range(blocks + 1, chunks):
        send_latent(c)
    w_in[2].wait()
    for lo in range(0, half, 256):
        part = dot(ranked[...], wqkv[:, lo : lo + 256]).astype(BF16)
        query[:, :, lo : lo + 256] = part.reshape(blocks, block_len, 256)
    for copy in w_in[3:]:
        copy.wait()

    same = lax.rem(lax.broadcasted_iota(jnp.int32, (rows, rows), 0), CHUNK) == lax.rem(
        lax.broadcasted_iota(jnp.int32, (rows, rows), 1), CHUNK
    )

    def temporal(c):
        own_copy(c).wait()

        @pl.loop(1, clip)
        def _(p):
            lat_copy(c, peer_of(p), peer_of(p)).wait_recv()

        normed = modulate(grp[c].reshape(rows, width), cond_ref)
        q = dot(normed, wqkv[:, half:width]).astype(BF16)
        k = dot(normed, wqkv[:, width + half : 2 * width]).astype(BF16)
        v = dot(normed, wqkv[:, 2 * width + half :]).astype(BF16)
        outs = []
        for h in range(sheads):
            cut = slice(h * head_dim, (h + 1) * head_dim)
            scores = jnp.where(same, dot_t(q[:, cut], k[:, cut]), -jnp.inf)
            expo = jnp.exp2((scores - jnp.max(scores, axis=-1, keepdims=True)) * scale)
            total = jnp.sum(expo, axis=-1, keepdims=True)
            outs.append((dot(expo.astype(BF16), v[:, cut]) / total).astype(BF16))
        result = jnp.concatenate(outs, axis=1).reshape(clip, CHUNK, half)
        t_out[c] = result
        tmp[c, rank] = t_out[c, rank]

        for p in far_first:
            ret_copy(c, peer_of(p), rank).start()

    pl.loop(0, chunks)(temporal)

    for kind, win in enumerate((kwin, vwin)):
        for side in range(2):

            @pl.loop(0, blocks)
            def _(b):
                halo_copy(win, kind, b, side).wait_recv()
    first_block = (me_s - 1) * blocks
    total_blocks = blocks * space_total

    @pl.loop(0, blocks)
    def _(b):
        ids = []
        for n in range(MAXNB):
            at = nb_ref[b, n] - first_block
            at = jnp.where(at >= total_blocks, at - total_blocks, at)
            at = jnp.where(at < 0, at + total_blocks, at)
            ids.append(jnp.clip(at, 0, 3 * blocks - 1))
        keys = [kwin[at] for at in ids]
        vals = [vwin[at] for at in ids]
        q = query[b]
        outs = []
        for h in range(sheads):
            cut = slice(h * head_dim, (h + 1) * head_dim)
            parts = []
            for n in range(MAXNB):
                part = dot_t(q[:, cut], keys[n][:, cut])
                if n > 0:
                    part = jnp.where(n < cnt_ref[b], part, -jnp.inf)
                parts.append(part)
            scores = jnp.concatenate(parts, axis=1)
            expo = jnp.exp2((scores - jnp.max(scores, axis=-1, keepdims=True)) * scale)
            total = jnp.sum(expo, axis=-1, keepdims=True)
            val = jnp.concatenate([vals[n][:, cut] for n in range(MAXNB)], axis=0)
            outs.append((dot(expo.astype(BF16), val) / total).astype(BF16))
        block_out[pl.ds(pl.multiple_of(b * block_len, block_len), block_len), :] = (
            jnp.concatenate(outs, axis=1)
        )

    spatial = dot(place[...], block_out[...]).astype(BF16)
    wout_in.wait()
    for lo in range(0, width, 256):
        part = dot(spatial, wout[:half, lo : lo + 256])
        sp_mixed[:, :, lo : lo + 256] = part.reshape(clip, per, 256)

    @pl.loop(0, chunks)
    def _(c):
        @pl.loop(1, clip)
        def _(p):
            ret_copy(c, peer_of(p), peer_of(p)).wait_recv()

        cut = pl.ds(pl.multiple_of(c * CHUNK, CHUNK), CHUNK)
        mixed = dot(tmp[c].reshape(rows, half), wout[half:, :]).reshape(clip, CHUNK, width)
        mixed = mixed + sp_mixed[:, cut, :]
        gate = cond_ref[2:3, :].reshape(1, 1, width)
        out_v[:, cut, :] = (lat[:, cut, :].astype(F32) + gate * mixed).astype(BF16)
        out_copy(c).start()

    @pl.loop(0, chunks)
    def _(c):
        out_copy(c).wait()

        @pl.loop(1, clip)
        def _(p):
            lat_copy(c, peer_of(p), rank).wait_send()
            ret_copy(c, peer_of(p), rank).wait_send()

    for kind, win in enumerate((kwin, vwin)):
        for side in range(2):

            @pl.loop(0, blocks)
            def _(b):
                halo_copy(win, kind, b, side).wait_send()


def body(latent, cond, w_qkv, w_out, slot, neighbours, counts):
    tokens, width = latent.shape[1], latent.shape[2]
    blocks = neighbours.shape[0]
    block_len = tokens // blocks
    half = width // 2
    clip = min(8, lax.axis_size("frame"))
    per = tokens // clip
    chunks = per // CHUNK
    hbm = pl.BlockSpec(memory_space=pltpu.HBM)
    dma = pltpu.SemaphoreType.DMA
    out = pl.pallas_call(
        functools.partial(kernel, clip),
        out_shape=jax.ShapeDtypeStruct((clip, per, width), BF16),
        in_specs=[hbm] * 7,
        out_specs=hbm,
        scratch_shapes=[
            pltpu.VMEM(cond.shape, F32),
            pltpu.VMEM((blocks, block_len), jnp.int32),
            pltpu.SMEM(neighbours.shape, jnp.int32),
            pltpu.SMEM(counts.shape, jnp.int32),
            pltpu.VMEM((clip, per, width), BF16),
            pltpu.VMEM(w_qkv.shape, BF16),
            pltpu.VMEM(w_out.shape, BF16),
            pltpu.VMEM((chunks, clip, CHUNK, width), BF16),
            pltpu.VMEM((tokens, width), BF16),
            pltpu.VMEM((tokens, width), BF16),
            pltpu.VMEM((blocks, block_len, half), BF16),
            pltpu.VMEM((3 * blocks, block_len, half), BF16),
            pltpu.VMEM((3 * blocks, block_len, half), BF16),
            pltpu.VMEM((tokens, tokens), BF16),
            pltpu.VMEM((tokens, half), BF16),
            pltpu.VMEM((clip, per, width), F32),
            pltpu.VMEM((chunks, clip, CHUNK, half), BF16),
            pltpu.VMEM((chunks, clip, CHUNK, half), BF16),
            pltpu.VMEM((clip, per, width), BF16),
            dma((7,)),
            dma((6,)),
            dma((chunks,)),
            dma((chunks, clip)),
            dma((chunks, clip)),
            dma((2, 2, blocks)),
            dma((2, 2, blocks)),
            dma((chunks, clip)),
            dma((chunks, clip)),
            dma((chunks,)),
        ],
        compiler_params=pltpu.CompilerParams(
            collective_id=0, has_side_effects=True, vmem_limit_bytes=48 * 1024 * 1024
        ),
        cost_estimate=pl.CostEstimate(
            flops=5_000_000_000, bytes_accessed=12_000_000, transcendentals=2_000_000
        ),
    )(
        *(
            pltpu.with_memory_space_constraint(x, pltpu.HBM)
            for x in (
                latent.reshape(clip, per, width),
                cond,
                w_qkv,
                w_out,
                slot.reshape(blocks, block_len),
                neighbours,
                counts,
            )
        )
    )
    return out.reshape(1, tokens, width)


def solution(mesh):
    in_specs = (P("frame", "space", None), P(), P(), P(), P("space"), P("space", None), P("space"))
    out_specs = P("frame", "space", None)
    return jax.shard_map(body, mesh=mesh, in_specs=in_specs, out_specs=out_specs, check_vma=False)
```

```python
import functools
import math

import jax
import jax.numpy as jnp
from jax import lax
from jax.experimental import pallas as pl
from jax.experimental.pallas import tpu as pltpu
from jax.sharding import PartitionSpec as P

HEADS = 8
MAXNB = 4
MESH = pl.DeviceIdType.MESH
F32 = jnp.float32
BF16 = jnp.bfloat16
CHUNK = 16


def modulate(rows, cond_ref):
    rows = rows.astype(F32)
    centred = rows - jnp.mean(rows, axis=-1, keepdims=True)
    normed = centred * lax.rsqrt(jnp.mean(centred * centred, axis=-1, keepdims=True) + 1e-06)
    return (normed * (1.0 + cond_ref[1:2, :]) + cond_ref[0:1, :]).astype(BF16)


def dot(a, b):
    return jnp.dot(a, b, preferred_element_type=F32)


def dot_t(a, b):
    return lax.dot_general(a, b, (((1,), (1,)), ((), ())), preferred_element_type=F32)


def kernel(
    clip,
    lat_hbm,
    cond_hbm,
    wqkv_hbm,
    wout_hbm,
    slot_hbm,
    nb_hbm,
    cnt_hbm,
    out_hbm,
    cond_ref,
    slot_ref,
    nb_ref,
    cnt_ref,
    lat,
    wqkv,
    wout,
    grp,
    mod,
    ranked,
    query,
    kwin,
    vwin,
    place,
    block_out,
    sp_mixed,
    t_out,
    tmp,
    out_v,
    local_sem,
    own_sem,
    lat_send,
    lat_recv,
    halo_send,
    halo_recv,
    ret_send,
    ret_recv,
    out_sem,
):
    space_total = lax.axis_size("space")
    me_s = lax.axis_index("space")
    me_f = lax.axis_index("frame")
    rank = lax.rem(me_f, clip)
    base = me_f - rank
    left = lax.rem(me_s + space_total - 1, space_total)
    right = lax.rem(me_s + 1, space_total)
    per, width = lat.shape[1], lat.shape[2]
    tokens = clip * per
    half = width // 2
    head_dim = width // HEADS
    sheads = HEADS // 2
    blocks, block_len = slot_ref.shape
    chunks = per // CHUNK
    rows = clip * CHUNK
    scale = math.log2(math.e) / math.sqrt(head_dim)

    far_first = sorted(range(1, clip), key=lambda p: abs(2 * p - clip))

    def peer_of(p):
        return lax.rem(rank + p, clip)

    lat_in = pltpu.make_async_copy(lat_hbm, lat, local_sem.at[0])
    wqkv_in = pltpu.make_async_copy(wqkv_hbm, wqkv, local_sem.at[1])
    wout_in = pltpu.make_async_copy(wout_hbm, wout, local_sem.at[2])
    small_in = [
        pltpu.make_async_copy(cond_hbm, cond_ref, local_sem.at[3]),
        pltpu.make_async_copy(slot_hbm, slot_ref, local_sem.at[4]),
        pltpu.make_async_copy(nb_hbm, nb_ref, local_sem.at[5]),
        pltpu.make_async_copy(cnt_hbm, cnt_ref, local_sem.at[6]),
    ]

    def own_copy(c):
        return pltpu.make_async_copy(
            lat_hbm.at[rank, pl.ds(pl.multiple_of(c * CHUNK, CHUNK), CHUNK)],
            grp.at[c, rank],
            own_sem.at[c],
        )

    def lat_copy(c, peer, slot):
        return pltpu.make_async_remote_copy(
            src_ref=lat_hbm.at[peer, pl.ds(pl.multiple_of(c * CHUNK, CHUNK), CHUNK)],
            dst_ref=grp.at[c, slot],
            send_sem=lat_send.at[c, peer],
            recv_sem=lat_recv.at[c, slot],
            device_id={"frame": base + peer},
            device_id_type=MESH,
        )

    def ret_copy(c, peer, slot):
        return pltpu.make_async_remote_copy(
            src_ref=t_out.at[c, peer],
            dst_ref=tmp.at[c, slot],
            send_sem=ret_send.at[c, peer],
            recv_sem=ret_recv.at[c, slot],
            device_id={"frame": base + peer},
            device_id_type=MESH,
        )

    def halo_copy(win, kind, part, side):
        at = part * (blocks // 2)
        return pltpu.make_async_remote_copy(
            src_ref=win.at[pl.ds(blocks + at, blocks // 2)],
            dst_ref=win.at[pl.ds(2 * blocks * side + at, blocks // 2)],
            send_sem=halo_send.at[kind, part, side],
            recv_sem=halo_recv.at[kind, part, side],
            device_id={"space": left if side else right},
            device_id_type=MESH,
        )

    def out_copy(c):
        cut = pl.ds(pl.multiple_of(c * CHUNK, CHUNK), CHUNK)
        return pltpu.make_async_copy(out_v.at[:, cut], out_hbm.at[:, cut], out_sem.at[c])

    barrier = pltpu.get_barrier_semaphore()

    @pl.loop(1, clip)
    def _(p):
        pl.semaphore_signal(
            barrier, inc=1, device_id={"frame": base + peer_of(p)}, device_id_type=MESH
        )

    for side in (left, right):
        pl.semaphore_signal(barrier, inc=1, device_id={"space": side}, device_id_type=MESH)
    lat_in.start()
    for copy in small_in:
        copy.start()
    wqkv_in.start()

    @pl.loop(0, chunks)
    def _(c):
        own_copy(c).start()

    pl.semaphore_wait(barrier, clip + 1)

    def send_latent(c):
        for p in far_first:
            lat_copy(c, peer_of(p), rank).start()

    send_latent(0)

    wout_in.start()
    for copy in small_in:
        copy.wait()
    lat_in.wait()

    @pl.loop(0, clip)
    def _(i):
        mod[pl.ds(pl.multiple_of(i * per, per), per), :] = modulate(lat[i], cond_ref)

    for b in range(blocks):
        cut = slice(b * block_len, (b + 1) * block_len)
        spots = lax.broadcasted_iota(jnp.int32, (tokens, block_len), 0)
        one_hot = jnp.where(spots == slot_ref[b : b + 1, :], 1.0, 0.0).astype(BF16)
        place[:, cut] = one_hot
        ranked[cut, :] = lax.dot_general(
            one_hot, mod[...], (((0,), (0,)), ((), ())), preferred_element_type=F32
        ).astype(BF16)

    wqkv_in.wait()
    for kind, win in enumerate((kwin, vwin)):
        for lo in range(0, half, 256):
            at = (kind + 1) * width + lo
            part = dot(ranked[...], wqkv[:, at : at + 256]).astype(BF16)
            win[blocks : 2 * blocks, :, lo : lo + 256] = part.reshape(blocks, block_len, 256)
        for part in range(2):
            for side in range(2):
                halo_copy(win, kind, part, side).start()
            step = 2 * kind + part + 1
            if step < chunks:
                send_latent(step)
    for c in range(5, chunks):
        send_latent(c)
    for lo in range(0, half, 256):
        part = dot(ranked[...], wqkv[:, lo : lo + 256]).astype(BF16)
        query[:, :, lo : lo + 256] = part.reshape(blocks, block_len, 256)

    same = lax.rem(lax.broadcasted_iota(jnp.int32, (rows, rows), 0), CHUNK) == lax.rem(
        lax.broadcasted_iota(jnp.int32, (rows, rows), 1), CHUNK
    )

    def send_result(c):
        for p in far_first:
            ret_copy(c, peer_of(p), rank).start()

    def temporal(c):
        own_copy(c).wait()

        @pl.loop(1, clip)
        def _(p):
            lat_copy(c, peer_of(p), peer_of(p)).wait_recv()

        @pl.when(c == chunks - 1)
        def _():
            pl.loop(0, chunks - 1)(send_result)

        normed = modulate(grp[c].reshape(rows, width), cond_ref)
        q = dot(normed, wqkv[:, half:width]).astype(BF16)
        k = dot(normed, wqkv[:, width + half : 2 * width]).astype(BF16)
        v = dot(normed, wqkv[:, 2 * width + half :]).astype(BF16)
        outs = []
        for h in range(sheads):
            cut = slice(h * head_dim, (h + 1) * head_dim)
            scores = jnp.where(same, dot_t(q[:, cut], k[:, cut]), -jnp.inf)
            expo = jnp.exp2((scores - jnp.max(scores, axis=-1, keepdims=True)) * scale)
            total = jnp.sum(expo, axis=-1, keepdims=True)
            outs.append((dot(expo.astype(BF16), v[:, cut]) / total).astype(BF16))
        result = jnp.concatenate(outs, axis=1).reshape(clip, CHUNK, half)
        t_out[c] = result
        tmp[c, rank] = t_out[c, rank]

    pl.loop(0, chunks)(temporal)
    send_result(chunks - 1)

    for kind, win in enumerate((kwin, vwin)):
        for part in range(2):
            for side in range(2):
                halo_copy(win, kind, part, side).wait_recv()
    first_block = (me_s - 1) * blocks
    total_blocks = blocks * space_total

    @pl.loop(0, blocks)
    def _(b):
        ids = []
        for n in range(MAXNB):
            at = nb_ref[b, n] - first_block
            at = jnp.where(at >= total_blocks, at - total_blocks, at)
            at = jnp.where(at < 0, at + total_blocks, at)
            ids.append(jnp.clip(at, 0, 3 * blocks - 1))
        keys = [kwin[at] for at in ids]
        vals = [vwin[at] for at in ids]
        q = query[b]
        outs = []
        for h in range(sheads):
            cut = slice(h * head_dim, (h + 1) * head_dim)
            parts = []
            for n in range(MAXNB):
                part = dot_t(q[:, cut], keys[n][:, cut])
                if n > 0:
                    part = jnp.where(n < cnt_ref[b], part, -jnp.inf)
                parts.append(part)
            scores = jnp.concatenate(parts, axis=1)
            expo = jnp.exp2((scores - jnp.max(scores, axis=-1, keepdims=True)) * scale)
            total = jnp.sum(expo, axis=-1, keepdims=True)
            val = jnp.concatenate([vals[n][:, cut] for n in range(MAXNB)], axis=0)
            outs.append((dot(expo.astype(BF16), val) / total).astype(BF16))
        block_out[pl.ds(pl.multiple_of(b * block_len, block_len), block_len), :] = (
            jnp.concatenate(outs, axis=1)
        )

    spatial = dot(place[...], block_out[...]).astype(BF16)
    wout_in.wait()
    for lo in range(0, width, 256):
        part = dot(spatial, wout[:half, lo : lo + 256])
        sp_mixed[:, :, lo : lo + 256] = part.reshape(clip, per, 256)

    @pl.loop(0, chunks)
    def _(c):
        @pl.loop(1, clip)
        def _(p):
            ret_copy(c, peer_of(p), peer_of(p)).wait_recv()

        cut = pl.ds(pl.multiple_of(c * CHUNK, CHUNK), CHUNK)
        mixed = dot(tmp[c].reshape(rows, half), wout[half:, :]).reshape(clip, CHUNK, width)
        mixed = mixed + sp_mixed[:, cut, :]
        gate = cond_ref[2:3, :].reshape(1, 1, width)
        out_v[:, cut, :] = (lat[:, cut, :].astype(F32) + gate * mixed).astype(BF16)
        out_copy(c).start()

    @pl.loop(0, chunks)
    def _(c):
        out_copy(c).wait()

        @pl.loop(1, clip)
        def _(p):
            lat_copy(c, peer_of(p), rank).wait_send()
            ret_copy(c, peer_of(p), rank).wait_send()

    for kind, win in enumerate((kwin, vwin)):
        for part in range(2):
            for side in range(2):
                halo_copy(win, kind, part, side).wait_send()


def body(latent, cond, w_qkv, w_out, slot, neighbours, counts):
    tokens, width = latent.shape[1], latent.shape[2]
    blocks = neighbours.shape[0]
    block_len = tokens // blocks
    half = width // 2
    clip = min(8, lax.axis_size("frame"))
    per = tokens // clip
    chunks = per // CHUNK
    hbm = pl.BlockSpec(memory_space=pltpu.HBM)
    dma = pltpu.SemaphoreType.DMA
    out = pl.pallas_call(
        functools.partial(kernel, clip),
        out_shape=jax.ShapeDtypeStruct((clip, per, width), BF16),
        in_specs=[hbm] * 7,
        out_specs=hbm,
        scratch_shapes=[
            pltpu.VMEM(cond.shape, F32),
            pltpu.VMEM((blocks, block_len), jnp.int32),
            pltpu.SMEM(neighbours.shape, jnp.int32),
            pltpu.SMEM(counts.shape, jnp.int32),
            pltpu.VMEM((clip, per, width), BF16),
            pltpu.VMEM(w_qkv.shape, BF16),
            pltpu.VMEM(w_out.shape, BF16),
            pltpu.VMEM((chunks, clip, CHUNK, width), BF16),
            pltpu.VMEM((tokens, width), BF16),
            pltpu.VMEM((tokens, width), BF16),
            pltpu.VMEM((blocks, block_len, half), BF16),
            pltpu.VMEM((3 * blocks, block_len, half), BF16),
            pltpu.VMEM((3 * blocks, block_len, half), BF16),
            pltpu.VMEM((tokens, tokens), BF16),
            pltpu.VMEM((tokens, half), BF16),
            pltpu.VMEM((clip, per, width), F32),
            pltpu.VMEM((chunks, clip, CHUNK, half), BF16),
            pltpu.VMEM((chunks, clip, CHUNK, half), BF16),
            pltpu.VMEM((clip, per, width), BF16),
            dma((7,)),
            dma((chunks,)),
            dma((chunks, clip)),
            dma((chunks, clip)),
            dma((2, 2, 2)),
            dma((2, 2, 2)),
            dma((chunks, clip)),
            dma((chunks, clip)),
            dma((chunks,)),
        ],
        compiler_params=pltpu.CompilerParams(
            collective_id=0, has_side_effects=True, vmem_limit_bytes=48 * 1024 * 1024
        ),
        cost_estimate=pl.CostEstimate(
            flops=5_000_000_000, bytes_accessed=12_000_000, transcendentals=2_000_000
        ),
    )(
        *(
            pltpu.with_memory_space_constraint(x, pltpu.HBM)
            for x in (
                latent.reshape(clip, per, width),
                cond,
                w_qkv,
                w_out,
                slot.reshape(blocks, block_len),
                neighbours,
                counts,
            )
        )
    )
    return out.reshape(1, tokens, width)


def solution(mesh):
    in_specs = (P("frame", "space", None), P(), P(), P(), P("space"), P("space", None), P("space"))
    out_specs = P("frame", "space", None)
    return jax.shard_map(body, mesh=mesh, in_specs=in_specs, out_specs=out_specs, check_vma=False)
```

```python
import functools
import math

import jax
import jax.numpy as jnp
from jax import lax
from jax.experimental import pallas as pl
from jax.experimental.pallas import tpu as pltpu
from jax.sharding import PartitionSpec as P

HEADS = 8
MAXNB = 4
MESH = pl.DeviceIdType.MESH
F32 = jnp.float32
BF16 = jnp.bfloat16
CHUNK = 32
GROUP = 16


def modulate(rows, cond_ref):
    rows = rows.astype(F32)
    centred = rows - jnp.mean(rows, axis=-1, keepdims=True)
    normed = centred * lax.rsqrt(jnp.mean(centred * centred, axis=-1, keepdims=True) + 1e-06)
    return (normed * (1.0 + cond_ref[1:2, :]) + cond_ref[0:1, :]).astype(BF16)


def dot(a, b):
    return jnp.dot(a, b, preferred_element_type=F32)


def dot_t(a, b):
    return lax.dot_general(a, b, (((1,), (1,)), ((), ())), preferred_element_type=F32)


def kernel(
    clip,
    lat_hbm,
    cond_hbm,
    wqkv_hbm,
    wout_hbm,
    slot_hbm,
    nb_hbm,
    cnt_hbm,
    out_hbm,
    cond_ref,
    slot_ref,
    nb_ref,
    cnt_ref,
    lat,
    wqkv,
    wout,
    grp,
    mod,
    g_mod,
    ranked,
    query,
    kwin,
    vwin,
    place,
    block_out,
    sp_mixed,
    t_out,
    tmp,
    out_v,
    local_sem,
    own_sem,
    lat_send,
    lat_recv,
    halo_send,
    halo_recv,
    ret_send,
    ret_recv,
    out_sem,
):
    space_total = lax.axis_size("space")
    me_s = lax.axis_index("space")
    me_f = lax.axis_index("frame")
    rank = lax.rem(me_f, clip)
    base = me_f - rank
    left = lax.rem(me_s + space_total - 1, space_total)
    right = lax.rem(me_s + 1, space_total)
    per, width = lat.shape[1], lat.shape[2]
    tokens = clip * per
    half = width // 2
    head_dim = width // HEADS
    sheads = HEADS // 2
    blocks, block_len = slot_ref.shape
    chunks = per // CHUNK
    rows = clip * CHUNK
    group_rows = clip * GROUP
    scale = math.log2(math.e) / math.sqrt(head_dim)

    far_first = sorted(range(1, clip), key=lambda p: abs(2 * p - clip))

    def peer_of(p):
        return lax.rem(rank + p, clip)

    lat_in = pltpu.make_async_copy(lat_hbm, lat, local_sem.at[0])
    wqkv_in = pltpu.make_async_copy(wqkv_hbm, wqkv, local_sem.at[1])
    wout_in = pltpu.make_async_copy(wout_hbm, wout, local_sem.at[2])
    small_in = [
        pltpu.make_async_copy(cond_hbm, cond_ref, local_sem.at[3]),
        pltpu.make_async_copy(slot_hbm, slot_ref, local_sem.at[4]),
        pltpu.make_async_copy(nb_hbm, nb_ref, local_sem.at[5]),
        pltpu.make_async_copy(cnt_hbm, cnt_ref, local_sem.at[6]),
    ]

    def own_copy(c):
        return pltpu.make_async_copy(
            lat_hbm.at[rank, pl.ds(pl.multiple_of(c * CHUNK, CHUNK), CHUNK)],
            grp.at[c, rank],
            own_sem.at[c],
        )

    def lat_copy(c, peer, slot):
        return pltpu.make_async_remote_copy(
            src_ref=lat_hbm.at[peer, pl.ds(pl.multiple_of(c * CHUNK, CHUNK), CHUNK)],
            dst_ref=grp.at[c, slot],
            send_sem=lat_send.at[c, peer],
            recv_sem=lat_recv.at[c, slot],
            device_id={"frame": base + peer},
            device_id_type=MESH,
        )

    def ret_copy(c, peer, slot):
        return pltpu.make_async_remote_copy(
            src_ref=t_out.at[c, peer],
            dst_ref=tmp.at[c, slot],
            send_sem=ret_send.at[c, peer],
            recv_sem=ret_recv.at[c, slot],
            device_id={"frame": base + peer},
            device_id_type=MESH,
        )

    def halo_copy(win, kind, part, side):
        at = part * (blocks // 2)
        return pltpu.make_async_remote_copy(
            src_ref=win.at[pl.ds(blocks + at, blocks // 2)],
            dst_ref=win.at[pl.ds(2 * blocks * side + at, blocks // 2)],
            send_sem=halo_send.at[kind, part, side],
            recv_sem=halo_recv.at[kind, part, side],
            device_id={"space": left if side else right},
            device_id_type=MESH,
        )

    def out_copy(c):
        cut = pl.ds(pl.multiple_of(c * CHUNK, CHUNK), CHUNK)
        return pltpu.make_async_copy(out_v.at[:, cut], out_hbm.at[:, cut], out_sem.at[c])

    barrier = pltpu.get_barrier_semaphore()

    @pl.loop(1, clip)
    def _(p):
        pl.semaphore_signal(
            barrier, inc=1, device_id={"frame": base + peer_of(p)}, device_id_type=MESH
        )

    for side in (left, right):
        pl.semaphore_signal(barrier, inc=1, device_id={"space": side}, device_id_type=MESH)
    lat_in.start()
    for copy in small_in:
        copy.start()
    wqkv_in.start()

    @pl.loop(0, chunks)
    def _(c):
        own_copy(c).start()

    pl.semaphore_wait(barrier, clip + 1)

    def send_latent(c):
        for p in far_first:
            lat_copy(c, peer_of(p), rank).start()

    send_latent(0)

    wout_in.start()
    for copy in small_in:
        copy.wait()
    lat_in.wait()

    for i in range(clip):
        mod[i * per : (i + 1) * per, :] = modulate(lat[i], cond_ref)

    for b in range(blocks):
        cut = slice(b * block_len, (b + 1) * block_len)
        spots = lax.broadcasted_iota(jnp.int32, (tokens, block_len), 0)
        one_hot = jnp.where(spots == slot_ref[b : b + 1, :], 1.0, 0.0).astype(BF16)
        place[:, cut] = one_hot
        ranked[cut, :] = lax.dot_general(
            one_hot, mod[...], (((0,), (0,)), ((), ())), preferred_element_type=F32
        ).astype(BF16)

    wqkv_in.wait()
    for kind, win in enumerate((kwin, vwin)):
        for lo in range(0, half, 256):
            at = (kind + 1) * width + lo
            part = dot(ranked[...], wqkv[:, at : at + 256]).astype(BF16)
            win[blocks : 2 * blocks, :, lo : lo + 256] = part.reshape(blocks, block_len, 256)
        for part in range(2):
            for side in range(2):
                halo_copy(win, kind, part, side).start()
            step = 2 * kind + part + 1
            if step < chunks:
                send_latent(step)
    for c in range(5, chunks):
        send_latent(c)
    for lo in range(0, half, 256):
        part = dot(ranked[...], wqkv[:, lo : lo + 256]).astype(BF16)
        query[:, :, lo : lo + 256] = part.reshape(blocks, block_len, 256)

    square = (group_rows, group_rows)
    same = lax.rem(lax.broadcasted_iota(jnp.int32, square, 0), GROUP) == lax.rem(
        lax.broadcasted_iota(jnp.int32, square, 1), GROUP
    )

    def send_result(c):
        for p in far_first:
            ret_copy(c, peer_of(p), rank).start()

    def temporal(c):
        own_copy(c).wait()

        @pl.loop(1, clip)
        def _(p):
            lat_copy(c, peer_of(p), peer_of(p)).wait_recv()

        @pl.when(c == chunks - 1)
        def _():
            pl.loop(0, chunks - 1)(send_result)

        for i in range(clip):
            g_mod[i * CHUNK : (i + 1) * CHUNK, :] = modulate(grp[c, i], cond_ref)
        normed = g_mod[...]
        q, k, v = (
            dot(normed, wqkv[:, at : at + half]).astype(BF16).reshape(clip, CHUNK, half)
            for at in (half, width + half, 2 * width + half)
        )
        for u in range(0, CHUNK, GROUP):
            for h in range(sheads):
                cut = slice(h * head_dim, (h + 1) * head_dim)
                one_q, one_k, one_v = (
                    x[:, u : u + GROUP, cut].reshape(group_rows, head_dim) for x in (q, k, v)
                )
                scores = jnp.where(same, dot_t(one_q, one_k), -jnp.inf)
                expo = jnp.exp2((scores - jnp.max(scores, axis=-1, keepdims=True)) * scale)
                total = jnp.sum(expo, axis=-1, keepdims=True)
                result = (dot(expo.astype(BF16), one_v) / total).astype(BF16)
                t_out[c, :, u : u + GROUP, cut] = result.reshape(clip, GROUP, head_dim)
        tmp[c, rank] = t_out[c, rank]

    pl.loop(0, chunks)(temporal)
    send_result(chunks - 1)

    for kind, win in enumerate((kwin, vwin)):
        for part in range(2):
            for side in range(2):
                halo_copy(win, kind, part, side).wait_recv()
    first_block = (me_s - 1) * blocks
    total_blocks = blocks * space_total

    @pl.loop(0, blocks)
    def _(b):
        ids = []
        for n in range(MAXNB):
            at = nb_ref[b, n] - first_block
            at = jnp.where(at >= total_blocks, at - total_blocks, at)
            at = jnp.where(at < 0, at + total_blocks, at)
            ids.append(jnp.clip(at, 0, 3 * blocks - 1))
        at_rows = pl.ds(pl.multiple_of(b * block_len, block_len), block_len)
        for h in range(sheads):
            cut = slice(h * head_dim, (h + 1) * head_dim)
            q = query[b, :, cut]
            parts = []
            for n in range(MAXNB):
                part = dot_t(q, kwin[ids[n], :, cut])
                if n > 0:
                    part = jnp.where(n < cnt_ref[b], part, -jnp.inf)
                parts.append(part)
            scores = jnp.concatenate(parts, axis=1)
            expo = jnp.exp2((scores - jnp.max(scores, axis=-1, keepdims=True)) * scale)
            total = jnp.sum(expo, axis=-1, keepdims=True)
            val = jnp.concatenate([vwin[at, :, cut] for at in ids], axis=0)
            block_out[at_rows, cut] = (dot(expo.astype(BF16), val) / total).astype(BF16)

    spatial = dot(place[...], block_out[...]).astype(BF16)
    wout_in.wait()
    for lo in range(0, width, 256):
        part = dot(spatial, wout[:half, lo : lo + 256])
        sp_mixed[:, :, lo : lo + 256] = part.reshape(clip, per, 256)

    @pl.loop(0, chunks)
    def _(c):
        @pl.loop(1, clip)
        def _(p):
            ret_copy(c, peer_of(p), peer_of(p)).wait_recv()

        cut = pl.ds(pl.multiple_of(c * CHUNK, CHUNK), CHUNK)
        mixed = dot(tmp[c].reshape(rows, half), wout[half:, :]).reshape(clip, CHUNK, width)
        mixed = mixed + sp_mixed[:, cut, :]
        gate = cond_ref[2:3, :].reshape(1, 1, width)
        out_v[:, cut, :] = (lat[:, cut, :].astype(F32) + gate * mixed).astype(BF16)
        out_copy(c).start()

    @pl.loop(0, chunks)
    def _(c):
        out_copy(c).wait()

        @pl.loop(1, clip)
        def _(p):
            lat_copy(c, peer_of(p), rank).wait_send()
            ret_copy(c, peer_of(p), rank).wait_send()

    for kind, win in enumerate((kwin, vwin)):
        for part in range(2):
            for side in range(2):
                halo_copy(win, kind, part, side).wait_send()


def body(latent, cond, w_qkv, w_out, slot, neighbours, counts):
    tokens, width = latent.shape[1], latent.shape[2]
    blocks = neighbours.shape[0]
    block_len = tokens // blocks
    half = width // 2
    clip = min(8, lax.axis_size("frame"))
    per = tokens // clip
    chunks = per // CHUNK
    hbm = pl.BlockSpec(memory_space=pltpu.HBM)
    dma = pltpu.SemaphoreType.DMA
    out = pl.pallas_call(
        functools.partial(kernel, clip),
        out_shape=jax.ShapeDtypeStruct((clip, per, width), BF16),
        in_specs=[hbm] * 7,
        out_specs=hbm,
        scratch_shapes=[
            pltpu.VMEM(cond.shape, F32),
            pltpu.VMEM((blocks, block_len), jnp.int32),
            pltpu.SMEM(neighbours.shape, jnp.int32),
            pltpu.SMEM(counts.shape, jnp.int32),
            pltpu.VMEM((clip, per, width), BF16),
            pltpu.VMEM(w_qkv.shape, BF16),
            pltpu.VMEM(w_out.shape, BF16),
            pltpu.VMEM((chunks, clip, CHUNK, width), BF16),
            pltpu.VMEM((tokens, width), BF16),
            pltpu.VMEM((clip * CHUNK, width), BF16),
            pltpu.VMEM((tokens, width), BF16),
            pltpu.VMEM((blocks, block_len, half), BF16),
            pltpu.VMEM((3 * blocks, block_len, half), BF16),
            pltpu.VMEM((3 * blocks, block_len, half), BF16),
            pltpu.VMEM((tokens, tokens), BF16),
            pltpu.VMEM((tokens, half), BF16),
            pltpu.VMEM((clip, per, width), F32),
            pltpu.VMEM((chunks, clip, CHUNK, half), BF16),
            pltpu.VMEM((chunks, clip, CHUNK, half), BF16),
            pltpu.VMEM((clip, per, width), BF16),
            dma((7,)),
            dma((chunks,)),
            dma((chunks, clip)),
            dma((chunks, clip)),
            dma((2, 2, 2)),
            dma((2, 2, 2)),
            dma((chunks, clip)),
            dma((chunks, clip)),
            dma((chunks,)),
        ],
        compiler_params=pltpu.CompilerParams(
            collective_id=0, has_side_effects=True, vmem_limit_bytes=48 * 1024 * 1024
        ),
        cost_estimate=pl.CostEstimate(
            flops=5_000_000_000, bytes_accessed=12_000_000, transcendentals=2_000_000
        ),
    )(
        *(
            pltpu.with_memory_space_constraint(x, pltpu.HBM)
            for x in (
                latent.reshape(clip, per, width),
                cond,
                w_qkv,
                w_out,
                slot.reshape(blocks, block_len),
                neighbours,
                counts,
            )
        )
    )
    return out.reshape(1, tokens, width)


def solution(mesh):
    in_specs = (P("frame", "space", None), P(), P(), P(), P("space"), P("space", None), P("space"))
    out_specs = P("frame", "space", None)
    return jax.shard_map(body, mesh=mesh, in_specs=in_specs, out_specs=out_specs, check_vma=False)
```

```python
import functools
import math

import jax
import jax.numpy as jnp
from jax import lax
from jax.experimental import pallas as pl
from jax.experimental.pallas import tpu as pltpu
from jax.sharding import PartitionSpec as P

HEADS = 8
MAXNB = 4
MESH = pl.DeviceIdType.MESH
F32 = jnp.float32
BF16 = jnp.bfloat16
CHUNK = 32
GROUP = 16


def modulate(rows, cond_ref):
    rows = rows.astype(F32)
    centred = rows - jnp.mean(rows, axis=-1, keepdims=True)
    normed = centred * lax.rsqrt(jnp.mean(centred * centred, axis=-1, keepdims=True) + 1e-06)
    return (normed * (1.0 + cond_ref[1:2, :]) + cond_ref[0:1, :]).astype(BF16)


def dot(a, b):
    return jnp.dot(a, b, preferred_element_type=F32)


def dot_t(a, b):
    return lax.dot_general(a, b, (((1,), (1,)), ((), ())), preferred_element_type=F32)


def kernel(
    clip,
    lat_hbm,
    cond_hbm,
    wqkv_hbm,
    wout_hbm,
    slot_hbm,
    nb_hbm,
    cnt_hbm,
    out_hbm,
    cond_ref,
    slot_ref,
    nb_ref,
    cnt_ref,
    lat,
    wqkv,
    wout,
    grp,
    mod,
    g_mod,
    ranked,
    query,
    kwin,
    vwin,
    place,
    block_out,
    sp_mixed,
    t_out,
    tmp,
    out_v,
    local_sem,
    w_sem,
    own_sem,
    lat_send,
    lat_recv,
    halo_send,
    halo_recv,
    ret_send,
    ret_recv,
    out_sem,
):
    space_total = lax.axis_size("space")
    me_s = lax.axis_index("space")
    me_f = lax.axis_index("frame")
    rank = lax.rem(me_f, clip)
    base = me_f - rank
    left = lax.rem(me_s + space_total - 1, space_total)
    right = lax.rem(me_s + 1, space_total)
    per, width = lat.shape[1], lat.shape[2]
    tokens = clip * per
    half = width // 2
    head_dim = width // HEADS
    sheads = HEADS // 2
    blocks, block_len = slot_ref.shape
    chunks = per // CHUNK
    rows = clip * CHUNK
    group_rows = clip * GROUP
    scale = math.log2(math.e) / math.sqrt(head_dim)

    far_first = sorted(range(1, clip), key=lambda p: abs(2 * p - clip))

    def peer_of(p):
        return lax.rem(rank + p, clip)

    lat_in = pltpu.make_async_copy(lat_hbm, lat, local_sem.at[0])
    w_in = []
    for i, at in enumerate((2, 4, 0, 1, 3, 5)):
        cut = pl.ds(at * half, half)
        w_in.append(pltpu.make_async_copy(wqkv_hbm.at[:, cut], wqkv.at[:, cut], w_sem.at[i]))
    wout_in = pltpu.make_async_copy(wout_hbm, wout, local_sem.at[2])
    small_in = [
        pltpu.make_async_copy(cond_hbm, cond_ref, local_sem.at[3]),
        pltpu.make_async_copy(slot_hbm, slot_ref, local_sem.at[4]),
        pltpu.make_async_copy(nb_hbm, nb_ref, local_sem.at[5]),
        pltpu.make_async_copy(cnt_hbm, cnt_ref, local_sem.at[6]),
    ]

    def own_copy(c):
        return pltpu.make_async_copy(
            lat_hbm.at[rank, pl.ds(pl.multiple_of(c * CHUNK, CHUNK), CHUNK)],
            grp.at[c, rank],
            own_sem.at[c],
        )

    def lat_copy(c, peer, slot):
        return pltpu.make_async_remote_copy(
            src_ref=lat_hbm.at[peer, pl.ds(pl.multiple_of(c * CHUNK, CHUNK), CHUNK)],
            dst_ref=grp.at[c, slot],
            send_sem=lat_send.at[c, peer],
            recv_sem=lat_recv.at[c, slot],
            device_id={"frame": base + peer},
            device_id_type=MESH,
        )

    def ret_copy(c, peer, slot):
        return pltpu.make_async_remote_copy(
            src_ref=t_out.at[c, peer],
            dst_ref=tmp.at[c, slot],
            send_sem=ret_send.at[c, peer],
            recv_sem=ret_recv.at[c, slot],
            device_id={"frame": base + peer},
            device_id_type=MESH,
        )

    def halo_copy(win, kind, part, side):
        at = part * (blocks // 2)
        return pltpu.make_async_remote_copy(
            src_ref=win.at[pl.ds(blocks + at, blocks // 2)],
            dst_ref=win.at[pl.ds(2 * blocks * side + at, blocks // 2)],
            send_sem=halo_send.at[kind, part, side],
            recv_sem=halo_recv.at[kind, part, side],
            device_id={"space": left if side else right},
            device_id_type=MESH,
        )

    def out_copy(c):
        cut = pl.ds(pl.multiple_of(c * CHUNK, CHUNK), CHUNK)
        return pltpu.make_async_copy(out_v.at[:, cut], out_hbm.at[:, cut], out_sem.at[c])

    barrier = pltpu.get_barrier_semaphore()

    @pl.loop(1, clip)
    def _(p):
        pl.semaphore_signal(
            barrier, inc=1, device_id={"frame": base + peer_of(p)}, device_id_type=MESH
        )

    for side in (left, right):
        pl.semaphore_signal(barrier, inc=1, device_id={"space": side}, device_id_type=MESH)
    lat_in.start()
    for copy in small_in:
        copy.start()
    for copy in w_in:
        copy.start()

    @pl.loop(0, chunks)
    def _(c):
        own_copy(c).start()

    pl.semaphore_wait(barrier, clip + 1)

    def send_latent(c):
        for p in far_first:
            lat_copy(c, peer_of(p), rank).start()

    send_latent(0)

    wout_in.start()
    for copy in small_in:
        copy.wait()
    lat_in.wait()

    for i in range(clip):
        mod[i * per : (i + 1) * per, :] = modulate(lat[i], cond_ref)

    for b in range(blocks):
        cut = slice(b * block_len, (b + 1) * block_len)
        spots = lax.broadcasted_iota(jnp.int32, (tokens, block_len), 0)
        one_hot = jnp.where(spots == slot_ref[b : b + 1, :], 1.0, 0.0).astype(BF16)
        place[:, cut] = one_hot
        picked = lax.dot_general(
            one_hot, mod[...], (((0,), (0,)), ((), ())), preferred_element_type=F32
        ).astype(BF16)
        ranked[cut, :] = picked
        if b % 2 == 0:
            continue
        two = slice((b - 1) * block_len, (b + 1) * block_len)
        for kind, win in enumerate((kwin, vwin)):
            if b == 1:
                w_in[kind].wait()
            at = (kind + 1) * width
            part = dot(ranked[two, :], wqkv[:, at : at + half]).astype(BF16)
            win[blocks + b - 1 : blocks + b + 1] = part.reshape(2, block_len, half)
            for side in range(2):
                halo_copy(win, kind, b // 2, side).start()
        if (b + 1) // 2 < chunks:
            send_latent((b + 1) // 2)
    for c in range(blocks // 2 + 1, chunks):
        send_latent(c)
    w_in[2].wait()
    for lo in range(0, half, 256):
        part = dot(ranked[...], wqkv[:, lo : lo + 256]).astype(BF16)
        query[:, :, lo : lo + 256] = part.reshape(blocks, block_len, 256)
    for copy in w_in[3:]:
        copy.wait()

    square = (group_rows, group_rows)
    same = lax.rem(lax.broadcasted_iota(jnp.int32, square, 0), GROUP) == lax.rem(
        lax.broadcasted_iota(jnp.int32, square, 1), GROUP
    )

    def send_result(c):
        for p in far_first:
            ret_copy(c, peer_of(p), rank).start()

    def temporal(c):
        own_copy(c).wait()

        @pl.loop(1, clip)
        def _(p):
            lat_copy(c, peer_of(p), peer_of(p)).wait_recv()

        @pl.when(c == chunks - 1)
        def _():
            pl.loop(0, chunks - 1)(send_result)

        for i in range(clip):
            g_mod[i * CHUNK : (i + 1) * CHUNK, :] = modulate(grp[c, i], cond_ref)
        normed = g_mod[...]
        q, k, v = (
            dot(normed, wqkv[:, at : at + half]).astype(BF16).reshape(clip, CHUNK, half)
            for at in (half, width + half, 2 * width + half)
        )
        for u in range(0, CHUNK, GROUP):
            for h in range(sheads):
                cut = slice(h * head_dim, (h + 1) * head_dim)
                one_q, one_k, one_v = (
                    x[:, u : u + GROUP, cut].reshape(group_rows, head_dim) for x in (q, k, v)
                )
                scores = jnp.where(same, dot_t(one_q, one_k), -jnp.inf)
                expo = jnp.exp2((scores - jnp.max(scores, axis=-1, keepdims=True)) * scale)
                total = jnp.sum(expo, axis=-1, keepdims=True)
                result = (dot(expo.astype(BF16), one_v) / total).astype(BF16)
                t_out[c, :, u : u + GROUP, cut] = result.reshape(clip, GROUP, head_dim)
        tmp[c, rank] = t_out[c, rank]

    pl.loop(0, chunks)(temporal)
    send_result(chunks - 1)

    for kind, win in enumerate((kwin, vwin)):
        for part in range(2):
            for side in range(2):
                halo_copy(win, kind, part, side).wait_recv()
    first_block = (me_s - 1) * blocks
    total_blocks = blocks * space_total

    @pl.loop(0, blocks)
    def _(b):
        ids = []
        for n in range(MAXNB):
            at = nb_ref[b, n] - first_block
            at = jnp.where(at >= total_blocks, at - total_blocks, at)
            at = jnp.where(at < 0, at + total_blocks, at)
            ids.append(jnp.clip(at, 0, 3 * blocks - 1))
        at_rows = pl.ds(pl.multiple_of(b * block_len, block_len), block_len)
        for h in range(sheads):
            cut = slice(h * head_dim, (h + 1) * head_dim)
            q = query[b, :, cut]
            parts = []
            for n in range(MAXNB):
                part = dot_t(q, kwin[ids[n], :, cut])
                if n > 0:
                    part = jnp.where(n < cnt_ref[b], part, -jnp.inf)
                parts.append(part)
            scores = jnp.concatenate(parts, axis=1)
            expo = jnp.exp2((scores - jnp.max(scores, axis=-1, keepdims=True)) * scale)
            total = jnp.sum(expo, axis=-1, keepdims=True)
            val = jnp.concatenate([vwin[at, :, cut] for at in ids], axis=0)
            block_out[at_rows, cut] = (dot(expo.astype(BF16), val) / total).astype(BF16)

    spatial = dot(place[...], block_out[...]).astype(BF16)
    wout_in.wait()
    for lo in range(0, width, 256):
        part = dot(spatial, wout[:half, lo : lo + 256])
        sp_mixed[:, :, lo : lo + 256] = part.reshape(clip, per, 256)

    @pl.loop(0, chunks)
    def _(c):
        @pl.loop(1, clip)
        def _(p):
            ret_copy(c, peer_of(p), peer_of(p)).wait_recv()

        cut = pl.ds(pl.multiple_of(c * CHUNK, CHUNK), CHUNK)
        mixed = dot(tmp[c].reshape(rows, half), wout[half:, :]).reshape(clip, CHUNK, width)
        mixed = mixed + sp_mixed[:, cut, :]
        gate = cond_ref[2:3, :].reshape(1, 1, width)
        out_v[:, cut, :] = (lat[:, cut, :].astype(F32) + gate * mixed).astype(BF16)
        out_copy(c).start()

    @pl.loop(0, chunks)
    def _(c):
        out_copy(c).wait()

        @pl.loop(1, clip)
        def _(p):
            lat_copy(c, peer_of(p), rank).wait_send()
            ret_copy(c, peer_of(p), rank).wait_send()

    for kind, win in enumerate((kwin, vwin)):
        for part in range(2):
            for side in range(2):
                halo_copy(win, kind, part, side).wait_send()


def body(latent, cond, w_qkv, w_out, slot, neighbours, counts):
    tokens, width = latent.shape[1], latent.shape[2]
    blocks = neighbours.shape[0]
    block_len = tokens // blocks
    half = width // 2
    clip = min(8, lax.axis_size("frame"))
    per = tokens // clip
    chunks = per // CHUNK
    hbm = pl.BlockSpec(memory_space=pltpu.HBM)
    dma = pltpu.SemaphoreType.DMA
    out = pl.pallas_call(
        functools.partial(kernel, clip),
        out_shape=jax.ShapeDtypeStruct((clip, per, width), BF16),
        in_specs=[hbm] * 7,
        out_specs=hbm,
        scratch_shapes=[
            pltpu.VMEM(cond.shape, F32),
            pltpu.VMEM((blocks, block_len), jnp.int32),
            pltpu.SMEM(neighbours.shape, jnp.int32),
            pltpu.SMEM(counts.shape, jnp.int32),
            pltpu.VMEM((clip, per, width), BF16),
            pltpu.VMEM(w_qkv.shape, BF16),
            pltpu.VMEM(w_out.shape, BF16),
            pltpu.VMEM((chunks, clip, CHUNK, width), BF16),
            pltpu.VMEM((tokens, width), BF16),
            pltpu.VMEM((clip * CHUNK, width), BF16),
            pltpu.VMEM((tokens, width), BF16),
            pltpu.VMEM((blocks, block_len, half), BF16),
            pltpu.VMEM((3 * blocks, block_len, half), BF16),
            pltpu.VMEM((3 * blocks, block_len, half), BF16),
            pltpu.VMEM((tokens, tokens), BF16),
            pltpu.VMEM((tokens, half), BF16),
            pltpu.VMEM((clip, per, width), F32),
            pltpu.VMEM((chunks, clip, CHUNK, half), BF16),
            pltpu.VMEM((chunks, clip, CHUNK, half), BF16),
            pltpu.VMEM((clip, per, width), BF16),
            dma((7,)),
            dma((6,)),
            dma((chunks,)),
            dma((chunks, clip)),
            dma((chunks, clip)),
            dma((2, 2, 2)),
            dma((2, 2, 2)),
            dma((chunks, clip)),
            dma((chunks, clip)),
            dma((chunks,)),
        ],
        compiler_params=pltpu.CompilerParams(
            collective_id=0, has_side_effects=True, vmem_limit_bytes=48 * 1024 * 1024
        ),
        cost_estimate=pl.CostEstimate(
            flops=5_000_000_000, bytes_accessed=12_000_000, transcendentals=2_000_000
        ),
    )(
        *(
            pltpu.with_memory_space_constraint(x, pltpu.HBM)
            for x in (
                latent.reshape(clip, per, width),
                cond,
                w_qkv,
                w_out,
                slot.reshape(blocks, block_len),
                neighbours,
                counts,
            )
        )
    )
    return out.reshape(1, tokens, width)


def solution(mesh):
    in_specs = (P("frame", "space", None), P(), P(), P(), P("space"), P("space", None), P("space"))
    out_specs = P("frame", "space", None)
    return jax.shard_map(body, mesh=mesh, in_specs=in_specs, out_specs=out_specs, check_vma=False)
```

```python
import functools
import math

import jax
import jax.numpy as jnp
from jax import lax
from jax.experimental import pallas as pl
from jax.experimental.pallas import tpu as pltpu
from jax.sharding import PartitionSpec as P

HEADS = 8
MAXNB = 4
MESH = pl.DeviceIdType.MESH
F32 = jnp.float32
BF16 = jnp.bfloat16
CHUNK = 32
GROUP = 16


def modulate(rows, cond_ref):
    rows = rows.astype(F32)
    centred = rows - jnp.mean(rows, axis=-1, keepdims=True)
    normed = centred * lax.rsqrt(jnp.mean(centred * centred, axis=-1, keepdims=True) + 1e-06)
    return (normed * (1.0 + cond_ref[1:2, :]) + cond_ref[0:1, :]).astype(BF16)


def dot(a, b):
    return jnp.dot(a, b, preferred_element_type=F32)


def dot_t(a, b):
    return lax.dot_general(a, b, (((1,), (1,)), ((), ())), preferred_element_type=F32)


def kernel(
    clip,
    lat_hbm,
    cond_hbm,
    wqkv_hbm,
    wout_hbm,
    slot_hbm,
    nb_hbm,
    cnt_hbm,
    out_ref,
    cond_ref,
    slot_ref,
    nb_ref,
    cnt_ref,
    lat,
    wqkv,
    wout,
    grp,
    mod,
    g_mod,
    ranked,
    query,
    kwin,
    vwin,
    place,
    block_out,
    sp_mixed,
    t_out,
    tmp,
    local_sem,
    w_sem,
    own_sem,
    lat_send,
    lat_recv,
    halo_send,
    halo_recv,
    ret_send,
    ret_recv,
):
    space_total = lax.axis_size("space")
    me_s = lax.axis_index("space")
    me_f = lax.axis_index("frame")
    rank = lax.rem(me_f, clip)
    base = me_f - rank
    left = lax.rem(me_s + space_total - 1, space_total)
    right = lax.rem(me_s + 1, space_total)
    per, width = lat.shape[1], lat.shape[2]
    tokens = clip * per
    half = width // 2
    head_dim = width // HEADS
    sheads = HEADS // 2
    blocks, block_len = slot_ref.shape
    chunks = per // CHUNK
    rows = clip * CHUNK
    group_rows = clip * GROUP
    scale = math.log2(math.e) / math.sqrt(head_dim)

    far_first = sorted(range(1, clip), key=lambda p: abs(2 * p - clip))

    def peer_of(p):
        return lax.rem(rank + p, clip)

    lat_in = pltpu.make_async_copy(lat_hbm, lat, local_sem.at[0])
    w_in = []
    for i, at in enumerate((2, 4, 0, 1, 3, 5)):
        cut = pl.ds(at * half, half)
        w_in.append(pltpu.make_async_copy(wqkv_hbm.at[:, cut], wqkv.at[:, cut], w_sem.at[i]))
    wout_in = pltpu.make_async_copy(wout_hbm, wout, local_sem.at[2])
    small_in = [
        pltpu.make_async_copy(cond_hbm, cond_ref, local_sem.at[3]),
        pltpu.make_async_copy(slot_hbm, slot_ref, local_sem.at[4]),
        pltpu.make_async_copy(nb_hbm, nb_ref, local_sem.at[5]),
        pltpu.make_async_copy(cnt_hbm, cnt_ref, local_sem.at[6]),
    ]

    def own_copy(c):
        return pltpu.make_async_copy(
            lat_hbm.at[rank, pl.ds(pl.multiple_of(c * CHUNK, CHUNK), CHUNK)],
            grp.at[c, rank],
            own_sem.at[c],
        )

    def lat_copy(c, peer, slot):
        return pltpu.make_async_remote_copy(
            src_ref=lat_hbm.at[peer, pl.ds(pl.multiple_of(c * CHUNK, CHUNK), CHUNK)],
            dst_ref=grp.at[c, slot],
            send_sem=lat_send.at[c, peer],
            recv_sem=lat_recv.at[c, slot],
            device_id={"frame": base + peer},
            device_id_type=MESH,
        )

    def ret_copy(c, peer, slot):
        return pltpu.make_async_remote_copy(
            src_ref=t_out.at[c, peer],
            dst_ref=tmp.at[c, slot],
            send_sem=ret_send.at[c, peer],
            recv_sem=ret_recv.at[c, slot],
            device_id={"frame": base + peer},
            device_id_type=MESH,
        )

    def halo_copy(win, kind, part, side):
        at = part * (blocks // 2)
        return pltpu.make_async_remote_copy(
            src_ref=win.at[pl.ds(blocks + at, blocks // 2)],
            dst_ref=win.at[pl.ds(2 * blocks * side + at, blocks // 2)],
            send_sem=halo_send.at[kind, part, side],
            recv_sem=halo_recv.at[kind, part, side],
            device_id={"space": left if side else right},
            device_id_type=MESH,
        )

    barrier = pltpu.get_barrier_semaphore()

    @pl.loop(1, clip)
    def _(p):
        pl.semaphore_signal(
            barrier, inc=1, device_id={"frame": base + peer_of(p)}, device_id_type=MESH
        )

    for side in (left, right):
        pl.semaphore_signal(barrier, inc=1, device_id={"space": side}, device_id_type=MESH)
    lat_in.start()
    for copy in small_in:
        copy.start()
    for copy in w_in:
        copy.start()

    @pl.loop(0, chunks)
    def _(c):
        own_copy(c).start()

    pl.semaphore_wait(barrier, clip + 1)

    def send_latent(c):
        for p in far_first:
            lat_copy(c, peer_of(p), rank).start()

    send_latent(0)

    wout_in.start()
    for copy in small_in:
        copy.wait()
    lat_in.wait()

    for i in range(clip):
        mod[i * per : (i + 1) * per, :] = modulate(lat[i], cond_ref)

    for b in range(blocks):
        cut = slice(b * block_len, (b + 1) * block_len)
        spots = lax.broadcasted_iota(jnp.int32, (tokens, block_len), 0)
        one_hot = jnp.where(spots == slot_ref[b : b + 1, :], 1.0, 0.0).astype(BF16)
        place[:, cut] = one_hot
        picked = lax.dot_general(
            one_hot, mod[...], (((0,), (0,)), ((), ())), preferred_element_type=F32
        ).astype(BF16)
        ranked[cut, :] = picked
        if b % 2 == 0:
            continue
        two = slice((b - 1) * block_len, (b + 1) * block_len)
        for kind, win in enumerate((kwin, vwin)):
            if b == 1:
                w_in[kind].wait()
            at = (kind + 1) * width
            part = dot(ranked[two, :], wqkv[:, at : at + half]).astype(BF16)
            win[blocks + b - 1 : blocks + b + 1] = part.reshape(2, block_len, half)
            for side in range(2):
                halo_copy(win, kind, b // 2, side).start()
        if (b + 1) // 2 < chunks:
            send_latent((b + 1) // 2)
    for c in range(blocks // 2 + 1, chunks):
        send_latent(c)
    w_in[2].wait()
    for lo in range(0, half, 256):
        part = dot(ranked[...], wqkv[:, lo : lo + 256]).astype(BF16)
        query[:, :, lo : lo + 256] = part.reshape(blocks, block_len, 256)
    for copy in w_in[3:]:
        copy.wait()

    square = (group_rows, group_rows)
    same = lax.rem(lax.broadcasted_iota(jnp.int32, square, 0), GROUP) == lax.rem(
        lax.broadcasted_iota(jnp.int32, square, 1), GROUP
    )

    def send_result(c):
        for p in far_first:
            ret_copy(c, peer_of(p), rank).start()

    def temporal(c):
        own_copy(c).wait()

        @pl.when(c == chunks - 1)
        def _():
            @pl.loop(1, clip)
            def _(p):
                lat_copy(c, peer_of(p), rank).wait_send()

            pl.loop(0, chunks - 1)(send_result)

        @pl.loop(1, clip)
        def _(p):
            lat_copy(c, peer_of(p), peer_of(p)).wait_recv()

        for i in range(clip):
            g_mod[i * CHUNK : (i + 1) * CHUNK, :] = modulate(grp[c, i], cond_ref)
        normed = g_mod[...]
        q, k, v = (
            dot(normed, wqkv[:, at : at + half]).astype(BF16).reshape(clip, CHUNK, half)
            for at in (half, width + half, 2 * width + half)
        )
        for u in range(0, CHUNK, GROUP):
            for h in range(sheads):
                cut = slice(h * head_dim, (h + 1) * head_dim)
                one_q, one_k, one_v = (
                    x[:, u : u + GROUP, cut].reshape(group_rows, head_dim) for x in (q, k, v)
                )
                scores = jnp.where(same, dot_t(one_q, one_k), -jnp.inf)
                expo = jnp.exp2((scores - jnp.max(scores, axis=-1, keepdims=True)) * scale)
                total = jnp.sum(expo, axis=-1, keepdims=True)
                result = (dot(expo.astype(BF16), one_v) / total).astype(BF16)
                t_out[c, :, u : u + GROUP, cut] = result.reshape(clip, GROUP, head_dim)
        tmp[c, rank] = t_out[c, rank]

    pl.loop(0, chunks)(temporal)
    send_result(chunks - 1)

    for kind, win in enumerate((kwin, vwin)):
        for part in range(2):
            for side in range(2):
                halo_copy(win, kind, part, side).wait_recv()
    first_block = (me_s - 1) * blocks
    total_blocks = blocks * space_total

    @pl.loop(0, blocks)
    def _(b):
        ids = []
        for n in range(MAXNB):
            at = nb_ref[b, n] - first_block
            at = jnp.where(at >= total_blocks, at - total_blocks, at)
            at = jnp.where(at < 0, at + total_blocks, at)
            ids.append(jnp.clip(at, 0, 3 * blocks - 1))
        at_rows = pl.ds(pl.multiple_of(b * block_len, block_len), block_len)
        for h in range(sheads):
            cut = slice(h * head_dim, (h + 1) * head_dim)
            q = query[b, :, cut]
            parts = []
            for n in range(MAXNB):
                part = dot_t(q, kwin[ids[n], :, cut])
                if n > 0:
                    part = jnp.where(n < cnt_ref[b], part, -jnp.inf)
                parts.append(part)
            scores = jnp.concatenate(parts, axis=1)
            expo = jnp.exp2((scores - jnp.max(scores, axis=-1, keepdims=True)) * scale)
            total = jnp.sum(expo, axis=-1, keepdims=True)
            val = jnp.concatenate([vwin[at, :, cut] for at in ids], axis=0)
            block_out[at_rows, cut] = (dot(expo.astype(BF16), val) / total).astype(BF16)

    spatial = dot(place[...], block_out[...]).astype(BF16)
    wout_in.wait()
    for lo in range(0, width, 256):
        part = dot(spatial, wout[:half, lo : lo + 256])
        sp_mixed[:, :, lo : lo + 256] = part.reshape(clip, per, 256)

    @pl.loop(0, chunks)
    def _(c):
        @pl.loop(1, clip)
        def _(p):
            ret_copy(c, peer_of(p), peer_of(p)).wait_recv()

        cut = pl.ds(pl.multiple_of(c * CHUNK, CHUNK), CHUNK)
        mixed = dot(tmp[c].reshape(rows, half), wout[half:, :]).reshape(clip, CHUNK, width)
        mixed = mixed + sp_mixed[:, cut, :]
        gate = cond_ref[2:3, :].reshape(1, 1, width)
        out_ref[:, cut, :] = (lat[:, cut, :].astype(F32) + gate * mixed).astype(BF16)

    @pl.loop(0, chunks)
    def _(c):
        @pl.loop(1, clip)
        def _(p):
            ret_copy(c, peer_of(p), rank).wait_send()

    @pl.loop(0, chunks - 1)
    def _(c):
        @pl.loop(1, clip)
        def _(p):
            lat_copy(c, peer_of(p), rank).wait_send()

    for kind, win in enumerate((kwin, vwin)):
        for part in range(2):
            for side in range(2):
                halo_copy(win, kind, part, side).wait_send()


def body(latent, cond, w_qkv, w_out, slot, neighbours, counts):
    tokens, width = latent.shape[1], latent.shape[2]
    blocks = neighbours.shape[0]
    block_len = tokens // blocks
    half = width // 2
    clip = min(8, lax.axis_size("frame"))
    per = tokens // clip
    chunks = per // CHUNK
    hbm = pl.BlockSpec(memory_space=pltpu.HBM)
    dma = pltpu.SemaphoreType.DMA
    out = pl.pallas_call(
        functools.partial(kernel, clip),
        out_shape=jax.ShapeDtypeStruct((clip, per, width), BF16),
        in_specs=[hbm] * 7,
        out_specs=pl.BlockSpec(memory_space=pltpu.VMEM),
        scratch_shapes=[
            pltpu.VMEM(cond.shape, F32),
            pltpu.VMEM((blocks, block_len), jnp.int32),
            pltpu.SMEM(neighbours.shape, jnp.int32),
            pltpu.SMEM(counts.shape, jnp.int32),
            pltpu.VMEM((clip, per, width), BF16),
            pltpu.VMEM(w_qkv.shape, BF16),
            pltpu.VMEM(w_out.shape, BF16),
            pltpu.VMEM((chunks, clip, CHUNK, width), BF16),
            pltpu.VMEM((tokens, width), BF16),
            pltpu.VMEM((clip * CHUNK, width), BF16),
            pltpu.VMEM((tokens, width), BF16),
            pltpu.VMEM((blocks, block_len, half), BF16),
            pltpu.VMEM((3 * blocks, block_len, half), BF16),
            pltpu.VMEM((3 * blocks, block_len, half), BF16),
            pltpu.VMEM((tokens, tokens), BF16),
            pltpu.VMEM((tokens, half), BF16),
            pltpu.VMEM((clip, per, width), F32),
            pltpu.VMEM((chunks, clip, CHUNK, half), BF16),
            pltpu.VMEM((chunks, clip, CHUNK, half), BF16),
            dma((7,)),
            dma((6,)),
            dma((chunks,)),
            dma((chunks, clip)),
            dma((chunks, clip)),
            dma((2, 2, 2)),
            dma((2, 2, 2)),
            dma((chunks, clip)),
            dma((chunks, clip)),
        ],
        compiler_params=pltpu.CompilerParams(
            collective_id=0, has_side_effects=True, vmem_limit_bytes=48 * 1024 * 1024
        ),
        cost_estimate=pl.CostEstimate(
            flops=5_000_000_000, bytes_accessed=12_000_000, transcendentals=2_000_000
        ),
    )(
        *(
            pltpu.with_memory_space_constraint(x, pltpu.HBM)
            for x in (
                latent.reshape(clip, per, width),
                cond,
                w_qkv,
                w_out,
                slot.reshape(blocks, block_len),
                neighbours,
                counts,
            )
        )
    )
    return out.reshape(1, tokens, width)


def solution(mesh):
    in_specs = (P("frame", "space", None), P(), P(), P(), P("space"), P("space", None), P("space"))
    out_specs = P("frame", "space", None)
    return jax.shard_map(body, mesh=mesh, in_specs=in_specs, out_specs=out_specs, check_vma=False)
```

```python
import functools
import math

import jax
import jax.numpy as jnp
from jax import lax
from jax.experimental import pallas as pl
from jax.experimental.pallas import tpu as pltpu
from jax.sharding import PartitionSpec as P

HEADS = 8
MAXNB = 4
MESH = pl.DeviceIdType.MESH
F32 = jnp.float32
BF16 = jnp.bfloat16
CHUNK = 32
GROUP = 16


def modulate(rows, cond_ref):
    rows = rows.astype(F32)
    centred = rows - jnp.mean(rows, axis=-1, keepdims=True)
    normed = centred * lax.rsqrt(jnp.mean(centred * centred, axis=-1, keepdims=True) + 1e-06)
    return (normed * (1.0 + cond_ref[1:2, :]) + cond_ref[0:1, :]).astype(BF16)


def dot(a, b):
    return jnp.dot(a, b, preferred_element_type=F32)


def dot_t(a, b):
    return lax.dot_general(a, b, (((1,), (1,)), ((), ())), preferred_element_type=F32)


def kernel(
    clip,
    lat_hbm,
    cond_hbm,
    wqkv_hbm,
    wout_hbm,
    slot_hbm,
    nb_hbm,
    cnt_hbm,
    out_hbm,
    cond_ref,
    slot_ref,
    nb_ref,
    cnt_ref,
    lat,
    wqkv,
    wout,
    grp,
    mod,
    g_mod,
    ranked,
    query,
    kwin,
    vwin,
    kfar,
    vfar,
    place,
    block_out,
    sp_mixed,
    t_out,
    tmp,
    out_v,
    local_sem,
    w_sem,
    own_sem,
    lat_send,
    lat_recv,
    near_send,
    near_recv,
    far_send,
    far_recv,
    ret_send,
    ret_recv,
    out_sem,
):
    space_total = lax.axis_size("space")
    me_s = lax.axis_index("space")
    me_f = lax.axis_index("frame")
    rank = lax.rem(me_f, clip)
    base = me_f - rank
    left = lax.rem(me_s + space_total - 1, space_total)
    right = lax.rem(me_s + 1, space_total)
    per, width = lat.shape[1], lat.shape[2]
    tokens = clip * per
    half = width // 2
    head_dim = width // HEADS
    sheads = HEADS // 2
    blocks, block_len = slot_ref.shape
    chunks = per // CHUNK
    rows = clip * CHUNK
    group_rows = clip * GROUP
    scale = math.log2(math.e) / math.sqrt(head_dim)

    far_first = sorted(range(1, clip), key=lambda p: abs(2 * p - clip))

    def peer_of(p):
        return lax.rem(rank + p, clip)

    lat_in = pltpu.make_async_copy(lat_hbm, lat, local_sem.at[0])
    w_in = []
    for i, at in enumerate((2, 4, 0, 1, 3, 5)):
        cut = pl.ds(at * half, half)
        w_in.append(pltpu.make_async_copy(wqkv_hbm.at[:, cut], wqkv.at[:, cut], w_sem.at[i]))
    wout_in = pltpu.make_async_copy(wout_hbm, wout, local_sem.at[2])
    small_in = [
        pltpu.make_async_copy(cond_hbm, cond_ref, local_sem.at[3]),
        pltpu.make_async_copy(slot_hbm, slot_ref, local_sem.at[4]),
        pltpu.make_async_copy(nb_hbm, nb_ref, local_sem.at[5]),
        pltpu.make_async_copy(cnt_hbm, cnt_ref, local_sem.at[6]),
    ]

    def own_copy(c):
        return pltpu.make_async_copy(
            lat_hbm.at[rank, pl.ds(pl.multiple_of(c * CHUNK, CHUNK), CHUNK)],
            grp.at[c, rank],
            own_sem.at[c],
        )

    def lat_copy(c, peer, slot):
        return pltpu.make_async_remote_copy(
            src_ref=lat_hbm.at[peer, pl.ds(pl.multiple_of(c * CHUNK, CHUNK), CHUNK)],
            dst_ref=grp.at[c, slot],
            send_sem=lat_send.at[c, peer],
            recv_sem=lat_recv.at[c, slot],
            device_id={"frame": base + peer},
            device_id_type=MESH,
        )

    def ret_copy(c, peer, slot):
        return pltpu.make_async_remote_copy(
            src_ref=t_out.at[c, peer],
            dst_ref=tmp.at[c, slot],
            send_sem=ret_send.at[c, peer],
            recv_sem=ret_recv.at[c, slot],
            device_id={"frame": base + peer},
            device_id_type=MESH,
        )

    odd = lax.rem(me_s, 2)
    near = jnp.where(odd == 1, left, right)
    far = jnp.where(odd == 1, right, left)

    def in_order(i, count, flip):
        return jnp.where(flip, count - 1 - i, i)

    def near_copy(win, kind, pair):
        return pltpu.make_async_remote_copy(
            src_ref=win.at[pl.ds(blocks + 2 * pair, 2)],
            dst_ref=win.at[pl.ds(2 * blocks * odd + 2 * pair, 2)],
            send_sem=near_send.at[kind, pair],
            recv_sem=near_recv.at[kind, pair],
            device_id={"space": near},
            device_id_type=MESH,
        )

    def far_copy(win, land, kind, b):
        return pltpu.make_async_remote_copy(
            src_ref=win.at[blocks + b],
            dst_ref=land.at[b],
            send_sem=far_send.at[kind, b],
            recv_sem=far_recv.at[kind, b],
            device_id={"space": far},
            device_id_type=MESH,
        )

    def out_copy(c):
        cut = pl.ds(pl.multiple_of(c * CHUNK, CHUNK), CHUNK)
        return pltpu.make_async_copy(out_v.at[:, cut], out_hbm.at[:, cut], out_sem.at[c])

    barrier = pltpu.get_barrier_semaphore()

    @pl.loop(1, clip)
    def _(p):
        pl.semaphore_signal(
            barrier, inc=1, device_id={"frame": base + peer_of(p)}, device_id_type=MESH
        )

    for side in (left, right):
        pl.semaphore_signal(barrier, inc=1, device_id={"space": side}, device_id_type=MESH)
    lat_in.start()
    for copy in small_in:
        copy.start()
    for copy in w_in:
        copy.start()

    @pl.loop(0, chunks)
    def _(c):
        own_copy(c).start()

    pl.semaphore_wait(barrier, clip + 1)

    def send_latent(c):
        for p in far_first:
            lat_copy(c, peer_of(p), rank).start()

    send_latent(0)

    wout_in.start()
    for copy in small_in:
        copy.wait()
    lat_in.wait()

    for i in range(clip):
        mod[i * per : (i + 1) * per, :] = modulate(lat[i], cond_ref)

    for b in range(blocks):
        spots = lax.broadcasted_iota(jnp.int32, (tokens, block_len), 0)
        one_hot = jnp.where(spots == slot_ref[b : b + 1, :], 1.0, 0.0).astype(BF16)
        place[:, b * block_len : (b + 1) * block_len] = one_hot
    two = 2 * block_len
    for step in range(blocks // 2):
        pair = in_order(step, blocks // 2, odd == 1)
        cut = pl.ds(pl.multiple_of(pair * two, two), two)
        ranked[cut, :] = lax.dot_general(
            place[:, cut], mod[...], (((0,), (0,)), ((), ())), preferred_element_type=F32
        ).astype(BF16)
        for kind, win in enumerate((kwin, vwin)):
            if step == 0:
                w_in[kind].wait()
            at = (kind + 1) * width
            part = dot(ranked[cut, :], wqkv[:, at : at + half]).astype(BF16)
            win[pl.ds(blocks + 2 * pair, 2)] = part.reshape(2, block_len, half)
        for j in range(2):
            b = 2 * pair + in_order(j, 2, odd == 1)
            far_copy(kwin, kfar, 0, b).start()
            far_copy(vwin, vfar, 1, b).start()
        near_copy(kwin, 0, pair).start()
        near_copy(vwin, 1, pair).start()
        if step + 1 < chunks:
            send_latent(step + 1)
    for c in range(blocks // 2 + 1, chunks):
        send_latent(c)
    w_in[2].wait()
    for lo in range(0, half, 256):
        part = dot(ranked[...], wqkv[:, lo : lo + 256]).astype(BF16)
        query[:, :, lo : lo + 256] = part.reshape(blocks, block_len, 256)
    for copy in w_in[3:]:
        copy.wait()

    square = (group_rows, group_rows)
    same = lax.rem(lax.broadcasted_iota(jnp.int32, square, 0), GROUP) == lax.rem(
        lax.broadcasted_iota(jnp.int32, square, 1), GROUP
    )

    def send_result(c):
        for p in far_first:
            ret_copy(c, peer_of(p), rank).start()

    def temporal(c):
        own_copy(c).wait()

        @pl.loop(1, clip)
        def _(p):
            lat_copy(c, peer_of(p), peer_of(p)).wait_recv()

        @pl.when(c == chunks - 1)
        def _():
            pl.loop(0, chunks - 1)(send_result)

        for i in range(clip):
            g_mod[i * CHUNK : (i + 1) * CHUNK, :] = modulate(grp[c, i], cond_ref)
        normed = g_mod[...]
        q, k, v = (
            dot(normed, wqkv[:, at : at + half]).astype(BF16).reshape(clip, CHUNK, half)
            for at in (half, width + half, 2 * width + half)
        )
        for u in range(0, CHUNK, GROUP):
            for h in range(sheads):
                cut = slice(h * head_dim, (h + 1) * head_dim)
                one_q, one_k, one_v = (
                    x[:, u : u + GROUP, cut].reshape(group_rows, head_dim) for x in (q, k, v)
                )
                scores = jnp.where(same, dot_t(one_q, one_k), -jnp.inf)
                expo = jnp.exp2((scores - jnp.max(scores, axis=-1, keepdims=True)) * scale)
                total = jnp.sum(expo, axis=-1, keepdims=True)
                result = (dot(expo.astype(BF16), one_v) / total).astype(BF16)
                t_out[c, :, u : u + GROUP, cut] = result.reshape(clip, GROUP, head_dim)
        tmp[c, rank] = t_out[c, rank]

    pl.loop(0, chunks)(temporal)
    send_result(chunks - 1)

    for kind, win in enumerate((kwin, vwin)):
        for pair in range(blocks // 2):
            near_copy(win, kind, pair).wait_recv()
    first_block = (me_s - 1) * blocks
    total_blocks = blocks * space_total

    @pl.loop(0, blocks)
    def _(i):
        b = in_order(i, blocks, odd == 0)
        for kind, (win, land) in enumerate(((kwin, kfar), (vwin, vfar))):
            far_copy(win, land, kind, b).wait_recv()
            win[2 * blocks * odd + b] = land[b]
        ids = []
        for n in range(MAXNB):
            at = nb_ref[b, n] - first_block
            at = jnp.where(at >= total_blocks, at - total_blocks, at)
            at = jnp.where(at < 0, at + total_blocks, at)
            ids.append(jnp.clip(at, 0, 3 * blocks - 1))
        at_rows = pl.ds(pl.multiple_of(b * block_len, block_len), block_len)
        for h in range(sheads):
            cut = slice(h * head_dim, (h + 1) * head_dim)
            q = query[b, :, cut]
            parts = []
            for n in range(MAXNB):
                part = dot_t(q, kwin[ids[n], :, cut])
                if n > 0:
                    part = jnp.where(n < cnt_ref[b], part, -jnp.inf)
                parts.append(part)
            scores = jnp.concatenate(parts, axis=1)
            expo = jnp.exp2((scores - jnp.max(scores, axis=-1, keepdims=True)) * scale)
            total = jnp.sum(expo, axis=-1, keepdims=True)
            val = jnp.concatenate([vwin[at, :, cut] for at in ids], axis=0)
            block_out[at_rows, cut] = (dot(expo.astype(BF16), val) / total).astype(BF16)

    spatial = dot(place[...], block_out[...]).astype(BF16)
    wout_in.wait()
    for lo in range(0, width, 256):
        part = dot(spatial, wout[:half, lo : lo + 256])
        sp_mixed[:, :, lo : lo + 256] = part.reshape(clip, per, 256)

    @pl.loop(0, chunks)
    def _(c):
        @pl.loop(1, clip)
        def _(p):
            ret_copy(c, peer_of(p), peer_of(p)).wait_recv()

        cut = pl.ds(pl.multiple_of(c * CHUNK, CHUNK), CHUNK)
        mixed = dot(tmp[c].reshape(rows, half), wout[half:, :]).reshape(clip, CHUNK, width)
        mixed = mixed + sp_mixed[:, cut, :]
        gate = cond_ref[2:3, :].reshape(1, 1, width)
        out_v[:, cut, :] = (lat[:, cut, :].astype(F32) + gate * mixed).astype(BF16)
        out_copy(c).start()

    @pl.loop(0, chunks)
    def _(c):
        out_copy(c).wait()

        @pl.loop(1, clip)
        def _(p):
            lat_copy(c, peer_of(p), rank).wait_send()
            ret_copy(c, peer_of(p), rank).wait_send()

    for kind, (win, land) in enumerate(((kwin, kfar), (vwin, vfar))):
        for pair in range(blocks // 2):
            near_copy(win, kind, pair).wait_send()
        for b in range(blocks):
            far_copy(win, land, kind, b).wait_send()


def body(latent, cond, w_qkv, w_out, slot, neighbours, counts):
    tokens, width = latent.shape[1], latent.shape[2]
    blocks = neighbours.shape[0]
    block_len = tokens // blocks
    half = width // 2
    clip = min(8, lax.axis_size("frame"))
    per = tokens // clip
    chunks = per // CHUNK
    hbm = pl.BlockSpec(memory_space=pltpu.HBM)
    dma = pltpu.SemaphoreType.DMA
    out = pl.pallas_call(
        functools.partial(kernel, clip),
        out_shape=jax.ShapeDtypeStruct((clip, per, width), BF16),
        in_specs=[hbm] * 7,
        out_specs=hbm,
        scratch_shapes=[
            pltpu.VMEM(cond.shape, F32),
            pltpu.VMEM((blocks, block_len), jnp.int32),
            pltpu.SMEM(neighbours.shape, jnp.int32),
            pltpu.SMEM(counts.shape, jnp.int32),
            pltpu.VMEM((clip, per, width), BF16),
            pltpu.VMEM(w_qkv.shape, BF16),
            pltpu.VMEM(w_out.shape, BF16),
            pltpu.VMEM((chunks, clip, CHUNK, width), BF16),
            pltpu.VMEM((tokens, width), BF16),
            pltpu.VMEM((clip * CHUNK, width), BF16),
            pltpu.VMEM((tokens, width), BF16),
            pltpu.VMEM((blocks, block_len, half), BF16),
            pltpu.VMEM((3 * blocks, block_len, half), BF16),
            pltpu.VMEM((3 * blocks, block_len, half), BF16),
            pltpu.VMEM((blocks, block_len, half), BF16),
            pltpu.VMEM((blocks, block_len, half), BF16),
            pltpu.VMEM((tokens, tokens), BF16),
            pltpu.VMEM((tokens, half), BF16),
            pltpu.VMEM((clip, per, width), F32),
            pltpu.VMEM((chunks, clip, CHUNK, half), BF16),
            pltpu.VMEM((chunks, clip, CHUNK, half), BF16),
            pltpu.VMEM((clip, per, width), BF16),
            dma((7,)),
            dma((6,)),
            dma((chunks,)),
            dma((chunks, clip)),
            dma((chunks, clip)),
            dma((2, blocks // 2)),
            dma((2, blocks // 2)),
            dma((2, blocks)),
            dma((2, blocks)),
            dma((chunks, clip)),
            dma((chunks, clip)),
            dma((chunks,)),
        ],
        compiler_params=pltpu.CompilerParams(
            collective_id=0, has_side_effects=True, vmem_limit_bytes=48 * 1024 * 1024
        ),
        cost_estimate=pl.CostEstimate(
            flops=5_000_000_000, bytes_accessed=12_000_000, transcendentals=2_000_000
        ),
    )(
        *(
            pltpu.with_memory_space_constraint(x, pltpu.HBM)
            for x in (
                latent.reshape(clip, per, width),
                cond,
                w_qkv,
                w_out,
                slot.reshape(blocks, block_len),
                neighbours,
                counts,
            )
        )
    )
    return out.reshape(1, tokens, width)


def solution(mesh):
    in_specs = (P("frame", "space", None), P(), P(), P(), P("space"), P("space", None), P("space"))
    out_specs = P("frame", "space", None)
    return jax.shard_map(body, mesh=mesh, in_specs=in_specs, out_specs=out_specs, check_vma=False)
```

```python
import functools
import math

import jax
import jax.numpy as jnp
from jax import lax
from jax.experimental import pallas as pl
from jax.experimental.pallas import tpu as pltpu
from jax.sharding import PartitionSpec as P

HEADS = 8
MAXNB = 4
MESH = pl.DeviceIdType.MESH
F32 = jnp.float32
BF16 = jnp.bfloat16
CHUNK = 32
GROUP = 16


def modulate(rows, cond_ref):
    rows = rows.astype(F32)
    centred = rows - jnp.mean(rows, axis=-1, keepdims=True)
    normed = centred * lax.rsqrt(jnp.mean(centred * centred, axis=-1, keepdims=True) + 1e-06)
    return (normed * (1.0 + cond_ref[1:2, :]) + cond_ref[0:1, :]).astype(BF16)


def dot(a, b):
    return jnp.dot(a, b, preferred_element_type=F32)


def dot_t(a, b):
    return lax.dot_general(a, b, (((1,), (1,)), ((), ())), preferred_element_type=F32)


def kernel(
    clip,
    lat_hbm,
    cond_hbm,
    wqkv_hbm,
    wout_hbm,
    slot_hbm,
    nb_hbm,
    cnt_hbm,
    out_ref,
    cond_ref,
    slot_ref,
    nb_ref,
    cnt_ref,
    lat,
    wqkv,
    wout,
    grp,
    mod,
    g_mod,
    ranked,
    query,
    kwin,
    vwin,
    kfar,
    vfar,
    place,
    block_out,
    sp_mixed,
    t_out,
    tmp,
    local_sem,
    w_sem,
    own_sem,
    lat_send,
    lat_recv,
    near_send,
    near_recv,
    far_send,
    far_recv,
    ret_send,
    ret_recv,
):
    space_total = lax.axis_size("space")
    me_s = lax.axis_index("space")
    me_f = lax.axis_index("frame")
    rank = lax.rem(me_f, clip)
    base = me_f - rank
    left = lax.rem(me_s + space_total - 1, space_total)
    right = lax.rem(me_s + 1, space_total)
    per, width = lat.shape[1], lat.shape[2]
    tokens = clip * per
    half = width // 2
    head_dim = width // HEADS
    sheads = HEADS // 2
    blocks, block_len = slot_ref.shape
    chunks = per // CHUNK
    rows = clip * CHUNK
    group_rows = clip * GROUP
    scale = math.log2(math.e) / math.sqrt(head_dim)

    far_first = sorted(range(1, clip), key=lambda p: abs(2 * p - clip))

    def peer_of(p):
        return lax.rem(rank + p, clip)

    lat_in = pltpu.make_async_copy(lat_hbm, lat, local_sem.at[0])
    w_in = []
    for i, at in enumerate((2, 4, 0, 1, 3, 5)):
        cut = pl.ds(at * half, half)
        w_in.append(pltpu.make_async_copy(wqkv_hbm.at[:, cut], wqkv.at[:, cut], w_sem.at[i]))
    wout_in = pltpu.make_async_copy(wout_hbm, wout, local_sem.at[2])
    small_in = [
        pltpu.make_async_copy(cond_hbm, cond_ref, local_sem.at[3]),
        pltpu.make_async_copy(slot_hbm, slot_ref, local_sem.at[4]),
        pltpu.make_async_copy(nb_hbm, nb_ref, local_sem.at[5]),
        pltpu.make_async_copy(cnt_hbm, cnt_ref, local_sem.at[6]),
    ]

    def own_copy(c):
        return pltpu.make_async_copy(
            lat_hbm.at[rank, pl.ds(pl.multiple_of(c * CHUNK, CHUNK), CHUNK)],
            grp.at[c, rank],
            own_sem.at[c],
        )

    def lat_copy(c, peer, slot):
        return pltpu.make_async_remote_copy(
            src_ref=lat_hbm.at[peer, pl.ds(pl.multiple_of(c * CHUNK, CHUNK), CHUNK)],
            dst_ref=grp.at[c, slot],
            send_sem=lat_send.at[c, peer],
            recv_sem=lat_recv.at[c, slot],
            device_id={"frame": base + peer},
            device_id_type=MESH,
        )

    def ret_copy(c, peer, slot):
        return pltpu.make_async_remote_copy(
            src_ref=t_out.at[c, peer],
            dst_ref=tmp.at[c, slot],
            send_sem=ret_send.at[c, peer],
            recv_sem=ret_recv.at[c, slot],
            device_id={"frame": base + peer},
            device_id_type=MESH,
        )

    odd = lax.rem(me_s, 2)
    near = jnp.where(odd == 1, left, right)
    far = jnp.where(odd == 1, right, left)

    def in_order(i, count, flip):
        return jnp.where(flip, count - 1 - i, i)

    def near_copy(win, kind, pair):
        return pltpu.make_async_remote_copy(
            src_ref=win.at[pl.ds(blocks + 2 * pair, 2)],
            dst_ref=win.at[pl.ds(2 * blocks * odd + 2 * pair, 2)],
            send_sem=near_send.at[kind, pair],
            recv_sem=near_recv.at[kind, pair],
            device_id={"space": near},
            device_id_type=MESH,
        )

    def far_copy(win, land, kind, b):
        return pltpu.make_async_remote_copy(
            src_ref=win.at[blocks + b],
            dst_ref=land.at[b],
            send_sem=far_send.at[kind, b],
            recv_sem=far_recv.at[kind, b],
            device_id={"space": far},
            device_id_type=MESH,
        )

    barrier = pltpu.get_barrier_semaphore()

    @pl.loop(1, clip)
    def _(p):
        pl.semaphore_signal(
            barrier, inc=1, device_id={"frame": base + peer_of(p)}, device_id_type=MESH
        )

    for side in (left, right):
        pl.semaphore_signal(barrier, inc=1, device_id={"space": side}, device_id_type=MESH)
    lat_in.start()
    for copy in small_in:
        copy.start()
    for copy in w_in:
        copy.start()

    @pl.loop(0, chunks)
    def _(c):
        own_copy(c).start()

    pl.semaphore_wait(barrier, clip + 1)

    def send_latent(c):
        for p in far_first:
            lat_copy(c, peer_of(p), rank).start()

    send_latent(0)

    wout_in.start()
    for copy in small_in:
        copy.wait()
    lat_in.wait()

    for i in range(clip):
        mod[i * per : (i + 1) * per, :] = modulate(lat[i], cond_ref)

    for b in range(blocks):
        spots = lax.broadcasted_iota(jnp.int32, (tokens, block_len), 0)
        one_hot = jnp.where(spots == slot_ref[b : b + 1, :], 1.0, 0.0).astype(BF16)
        place[:, b * block_len : (b + 1) * block_len] = one_hot
    two = 2 * block_len
    for step in range(blocks // 2):
        pair = in_order(step, blocks // 2, odd == 1)
        cut = pl.ds(pl.multiple_of(pair * two, two), two)
        ranked[cut, :] = lax.dot_general(
            place[:, cut], mod[...], (((0,), (0,)), ((), ())), preferred_element_type=F32
        ).astype(BF16)
        for kind, win in enumerate((kwin, vwin)):
            if step == 0:
                w_in[kind].wait()
            at = (kind + 1) * width
            part = dot(ranked[cut, :], wqkv[:, at : at + half]).astype(BF16)
            win[pl.ds(blocks + 2 * pair, 2)] = part.reshape(2, block_len, half)
        for j in range(2):
            b = 2 * pair + in_order(j, 2, odd == 1)
            far_copy(kwin, kfar, 0, b).start()
            far_copy(vwin, vfar, 1, b).start()
        near_copy(kwin, 0, pair).start()
        near_copy(vwin, 1, pair).start()
        if step + 1 < chunks:
            send_latent(step + 1)
    for c in range(blocks // 2 + 1, chunks):
        send_latent(c)
    w_in[2].wait()
    for lo in range(0, half, 256):
        part = dot(ranked[...], wqkv[:, lo : lo + 256]).astype(BF16)
        query[:, :, lo : lo + 256] = part.reshape(blocks, block_len, 256)
    for copy in w_in[3:]:
        copy.wait()

    square = (group_rows, group_rows)
    same = lax.rem(lax.broadcasted_iota(jnp.int32, square, 0), GROUP) == lax.rem(
        lax.broadcasted_iota(jnp.int32, square, 1), GROUP
    )

    def send_result(c):
        for p in far_first:
            ret_copy(c, peer_of(p), rank).start()

    def temporal(c):
        own_copy(c).wait()

        @pl.loop(1, clip)
        def _(p):
            lat_copy(c, peer_of(p), peer_of(p)).wait_recv()

        @pl.when(c == chunks - 1)
        def _():
            pl.loop(0, chunks - 1)(send_result)

        for i in range(clip):
            g_mod[i * CHUNK : (i + 1) * CHUNK, :] = modulate(grp[c, i], cond_ref)
        normed = g_mod[...]
        q, k, v = (
            dot(normed, wqkv[:, at : at + half]).astype(BF16).reshape(clip, CHUNK, half)
            for at in (half, width + half, 2 * width + half)
        )
        for u in range(0, CHUNK, GROUP):
            for h in range(sheads):
                cut = slice(h * head_dim, (h + 1) * head_dim)
                one_q, one_k, one_v = (
                    x[:, u : u + GROUP, cut].reshape(group_rows, head_dim) for x in (q, k, v)
                )
                scores = jnp.where(same, dot_t(one_q, one_k), -jnp.inf)
                expo = jnp.exp2((scores - jnp.max(scores, axis=-1, keepdims=True)) * scale)
                total = jnp.sum(expo, axis=-1, keepdims=True)
                result = (dot(expo.astype(BF16), one_v) / total).astype(BF16)
                t_out[c, :, u : u + GROUP, cut] = result.reshape(clip, GROUP, head_dim)
        tmp[c, rank] = t_out[c, rank]

    pl.loop(0, chunks)(temporal)
    send_result(chunks - 1)

    for kind, win in enumerate((kwin, vwin)):
        for pair in range(blocks // 2):
            near_copy(win, kind, pair).wait_recv()
    first_block = (me_s - 1) * blocks
    total_blocks = blocks * space_total

    @pl.loop(0, blocks)
    def _(i):
        b = in_order(i, blocks, odd == 0)
        for kind, (win, land) in enumerate(((kwin, kfar), (vwin, vfar))):
            far_copy(win, land, kind, b).wait_recv()
            win[2 * blocks * odd + b] = land[b]
        ids = []
        for n in range(MAXNB):
            at = nb_ref[b, n] - first_block
            at = jnp.where(at >= total_blocks, at - total_blocks, at)
            at = jnp.where(at < 0, at + total_blocks, at)
            ids.append(jnp.clip(at, 0, 3 * blocks - 1))
        at_rows = pl.ds(pl.multiple_of(b * block_len, block_len), block_len)
        for h in range(sheads):
            cut = slice(h * head_dim, (h + 1) * head_dim)
            q = query[b, :, cut]
            parts = []
            for n in range(MAXNB):
                part = dot_t(q, kwin[ids[n], :, cut])
                if n > 0:
                    part = jnp.where(n < cnt_ref[b], part, -jnp.inf)
                parts.append(part)
            scores = jnp.concatenate(parts, axis=1)
            expo = jnp.exp2((scores - jnp.max(scores, axis=-1, keepdims=True)) * scale)
            total = jnp.sum(expo, axis=-1, keepdims=True)
            val = jnp.concatenate([vwin[at, :, cut] for at in ids], axis=0)
            block_out[at_rows, cut] = (dot(expo.astype(BF16), val) / total).astype(BF16)

    spatial = dot(place[...], block_out[...]).astype(BF16)
    wout_in.wait()
    for lo in range(0, width, 256):
        part = dot(spatial, wout[:half, lo : lo + 256])
        sp_mixed[:, :, lo : lo + 256] = part.reshape(clip, per, 256)

    @pl.loop(0, chunks)
    def _(c):
        @pl.loop(1, clip)
        def _(p):
            ret_copy(c, peer_of(p), peer_of(p)).wait_recv()

        cut = pl.ds(pl.multiple_of(c * CHUNK, CHUNK), CHUNK)
        mixed = dot(tmp[c].reshape(rows, half), wout[half:, :]).reshape(clip, CHUNK, width)
        mixed = mixed + sp_mixed[:, cut, :]
        gate = cond_ref[2:3, :].reshape(1, 1, width)
        out_ref[:, cut, :] = (lat[:, cut, :].astype(F32) + gate * mixed).astype(BF16)

    @pl.loop(0, chunks)
    def _(c):
        @pl.loop(1, clip)
        def _(p):
            lat_copy(c, peer_of(p), rank).wait_send()
            ret_copy(c, peer_of(p), rank).wait_send()

    for kind, (win, land) in enumerate(((kwin, kfar), (vwin, vfar))):
        for pair in range(blocks // 2):
            near_copy(win, kind, pair).wait_send()
        for b in range(blocks):
            far_copy(win, land, kind, b).wait_send()


def body(latent, cond, w_qkv, w_out, slot, neighbours, counts):
    tokens, width = latent.shape[1], latent.shape[2]
    blocks = neighbours.shape[0]
    block_len = tokens // blocks
    half = width // 2
    clip = min(8, lax.axis_size("frame"))
    per = tokens // clip
    chunks = per // CHUNK
    hbm = pl.BlockSpec(memory_space=pltpu.HBM)
    dma = pltpu.SemaphoreType.DMA
    out = pl.pallas_call(
        functools.partial(kernel, clip),
        out_shape=jax.ShapeDtypeStruct((clip, per, width), BF16),
        in_specs=[hbm] * 7,
        out_specs=pl.BlockSpec(memory_space=pltpu.VMEM),
        scratch_shapes=[
            pltpu.VMEM(cond.shape, F32),
            pltpu.VMEM((blocks, block_len), jnp.int32),
            pltpu.SMEM(neighbours.shape, jnp.int32),
            pltpu.SMEM(counts.shape, jnp.int32),
            pltpu.VMEM((clip, per, width), BF16),
            pltpu.VMEM(w_qkv.shape, BF16),
            pltpu.VMEM(w_out.shape, BF16),
            pltpu.VMEM((chunks, clip, CHUNK, width), BF16),
            pltpu.VMEM((tokens, width), BF16),
            pltpu.VMEM((clip * CHUNK, width), BF16),
            pltpu.VMEM((tokens, width), BF16),
            pltpu.VMEM((blocks, block_len, half), BF16),
            pltpu.VMEM((3 * blocks, block_len, half), BF16),
            pltpu.VMEM((3 * blocks, block_len, half), BF16),
            pltpu.VMEM((blocks, block_len, half), BF16),
            pltpu.VMEM((blocks, block_len, half), BF16),
            pltpu.VMEM((tokens, tokens), BF16),
            pltpu.VMEM((tokens, half), BF16),
            pltpu.VMEM((clip, per, width), F32),
            pltpu.VMEM((chunks, clip, CHUNK, half), BF16),
            pltpu.VMEM((chunks, clip, CHUNK, half), BF16),
            dma((7,)),
            dma((6,)),
            dma((chunks,)),
            dma((chunks, clip)),
            dma((chunks, clip)),
            dma((2, blocks // 2)),
            dma((2, blocks // 2)),
            dma((2, blocks)),
            dma((2, blocks)),
            dma((chunks, clip)),
            dma((chunks, clip)),
        ],
        compiler_params=pltpu.CompilerParams(
            collective_id=0, has_side_effects=True, vmem_limit_bytes=48 * 1024 * 1024
        ),
        cost_estimate=pl.CostEstimate(
            flops=5_000_000_000, bytes_accessed=12_000_000, transcendentals=2_000_000
        ),
    )(
        *(
            pltpu.with_memory_space_constraint(x, pltpu.HBM)
            for x in (
                latent.reshape(clip, per, width),
                cond,
                w_qkv,
                w_out,
                slot.reshape(blocks, block_len),
                neighbours,
                counts,
            )
        )
    )
    return out.reshape(1, tokens, width)


def solution(mesh):
    in_specs = (P("frame", "space", None), P(), P(), P(), P("space"), P("space", None), P("space"))
    out_specs = P("frame", "space", None)
    return jax.shard_map(body, mesh=mesh, in_specs=in_specs, out_specs=out_specs, check_vma=False)
```
